256 devices in a mesh: dp: 64 (over y, z, core), tensor: 4 (over x).
Axes of the slice: x: 4, y: 4, z: 8, core: 2. Of those that a mesh axis runs over, the one named last changes fastest.
Arguments:
- tokens: bfloat16 [16384, 4096], P('dp', 'tensor'), may hold values from -6 to 6
- x_weight: bfloat16 [4096, 8192], P('dp', 'tensor'), may hold values from -0.09375 to 0.09375
- bc_weight: bfloat16 [4096, 512], P('dp', 'tensor'), may hold values from -0.0234375 to 0.0234375
- step_weight: bfloat16 [4096, 128], P('dp', 'tensor'), may hold values from -0.09375 to 0.09375
- step_bias: float32 [128], P('tensor'), may hold values from -2 to 1
- decay_log: float32 [128], P('tensor'), may hold values from -6 to -1.5
- skip_gain: float32 [128], P('tensor'), may hold values from 0.5 to 1.5
- queries: bfloat16 [16384, 4096], P('dp', 'tensor'), may hold values from -12 to 12
- new_keyvals: bfloat16 [16384, 1024], P('dp', 'tensor'), may hold values from -6 to 6
- page_pool: bfloat16 [6144, 128, 1024], P('dp', None, 'tensor'), may hold values from -6 to 6
- page_table: int32 [128, 48], P('dp'), may hold values from 0 to 6143, as said below
- prefix_pages: int32 [128], P('dp'), may hold values from 16 to 32
- new_counts: int32 [128], P('dp'), may hold values from 64 to 128
Outputs:
- mamba_out: bfloat16 [16384, 8192], P('dp', 'tensor')
- attention_out: bfloat16 [16384, 4096], P('dp', 'tensor')
The draws below stay inside these ranges and needn't reach their ends.
Inputs may be any that keep to these rules, and one draw needn't show every extreme that they name: `page_table`: row g lists sequence g's 16 state pages, then its 32 key-value page slots; every pool page is named exactly once; page id // 96 is its pool owner; the rows of one owner's 2 sequences name at most 2 pages of any one pool owner, of which at most 1 are state pages and at most 1 key-value pages.
All inputs are finite; a program needn't handle non-finite values.
Results may differ from the reference program's by a relative error of at most 0.0061.
Values may be sent and summed in bfloat16 or wider, within the bound.
No kernel may reach another device: no remote copies, remote signals or barrier semaphores. Data moves between devices by JAX's collectives and lax.ppermute only.
A program may use at most 192 MiB of HBM per device.

```python
import math
import jax
import jax.numpy as jnp
from jax import lax

D = 4096
MH = 128
HP = 64
NST = 256
AQ = 32
AKV = 4
HD = 128
PAGE = 128
MAXP = 32
SEQ_DEV = 2
NEW = 128
SP = 16
POOL = 96
SEQS = 128
TOKENS = 16384
N_DP = 64


def draw_page_table(key, part):
    key = jax.random.fold_in(key, 11)
    first, second, third = jax.random.split(key, 3)
    owners = SEQS // SEQ_DEV
    width = SP + MAXP
    relabel = jax.random.permutation(first, owners)
    inverse = jnp.argsort(relabel)
    shifts = jax.random.permutation(second, owners)
    column = jnp.arange(width)[None, :]
    within = jnp.arange(SEQ_DEV)[:, None]
    slot = jnp.where(column < SP, within * SP + column, SEQ_DEV * SP + within * MAXP + column - SP)
    offset = shifts[slot % owners]
    owner = jnp.arange(owners)[:, None, None]
    source = inverse[(relabel[owner] + offset[None, :, :]) % owners]
    orders = jax.vmap(lambda single: jax.random.permutation(single, POOL))(jax.random.split(third, owners))
    local = jnp.broadcast_to(slot[None, :, :], source.shape)
    pages = source * POOL + orders[source, local]
    return pages.reshape(SEQS, width).astype(jnp.int32)


def draw_prefix_pages(key, part):
    key = jax.random.fold_in(key, 5)
    first, second = jax.random.split(key)
    values = jax.random.randint(first, (SEQS,), MAXP // 2, MAXP + 1)
    chosen = jax.random.randint(second, (), 0, SEQS)
    return values.at[chosen].set(MAXP).astype(jnp.int32)


def draw_new_counts(key, part):
    key = jax.random.fold_in(key, 7)
    first, second = jax.random.split(key)
    values = jax.random.randint(first, (SEQS,), NEW // 2, NEW + 1)
    chosen = jax.random.randint(second, (), 0, SEQS)
    return values.at[chosen].set(NEW).astype(jnp.int32)


def draw_queries(key, part):
    key = jax.random.fold_in(key, 13)
    values = jnp.clip(2.5 * jax.random.normal(key, (TOKENS, AQ * HD), jnp.float32), -12.0, 12.0)
    return values.astype(jnp.bfloat16)


def draw_new_keyvals(key, part):
    key = jax.random.fold_in(key, 17)
    values = jnp.clip(jax.random.normal(key, (TOKENS, AKV * 2 * HD), jnp.float32), -6.0, 6.0)
    return values.astype(jnp.bfloat16)


def levels(stream_key, shape, pieces, least, largest):
    def one(axis_at, parts):
        heights = jax.random.uniform(jax.random.fold_in(jax.random.fold_in(stream_key, 6), axis_at), (parts,), jnp.float32, least / len(pieces), largest / len(pieces))
        return jnp.repeat(jnp.exp(heights), shape[axis_at] // parts).reshape((-1,) + (1,) * (len(shape) - axis_at - 1))

    factor_of = one(*pieces[0])
    for cut in pieces[1:]:
        factor_of = factor_of * one(*cut)
    return factor_of


def centred(stream_key, dims, scale, reach, shards=(), kind=jnp.bfloat16):
    entries = scale * jax.random.normal(stream_key, dims, jnp.float32)
    if shards:
        entries = entries * levels(stream_key, dims, shards, -0.22, 0.18)
    return jnp.clip(entries, -reach, reach).astype(kind)


def setup_inputs(seed: int = 0) -> dict:
    seeds = jax.random.split(jax.random.key(seed), 14)
    return {
        "tokens": centred(seeds[0], (TOKENS, D), 1.0, 6.0, ((0, 64), (1, 4))),
        "x_weight": centred(seeds[1], (D, MH * HP), D ** -0.5, 0.09375, ((0, 64), (1, 4))),
        "bc_weight": centred(seeds[2], (D, 2 * NST), (16 * D) ** -0.5, 0.0234375, ((0, 64), (1, 4))),
        "step_weight": centred(seeds[3], (D, MH), D ** -0.5, 0.09375, ((0, 64), (1, 4))),
        "step_bias": jnp.clip(-2.0 + 3.0 * jax.random.uniform(seeds[4], (MH,), jnp.float32) ** levels(seeds[4], (MH,), ((0, 4),), -0.2, 0.2), -2.0, 1.0),
        "decay_log": jnp.clip(-6.0 + 4.5 * jax.random.uniform(seeds[5], (MH,), jnp.float32) ** levels(seeds[5], (MH,), ((0, 4),), -0.2, 0.2), -6.0, -1.5),
        "skip_gain": jnp.clip(0.5 + 1.0 * jax.random.uniform(seeds[6], (MH,), jnp.float32) ** levels(seeds[6], (MH,), ((0, 4),), -0.2, 0.2), 0.5, 1.5),
        "queries": draw_queries(jax.random.fold_in(seeds[13], 71), 0),
        "new_keyvals": draw_new_keyvals(jax.random.fold_in(seeds[13], 71), 0),
        "page_pool": centred(seeds[9], (N_DP * POOL, PAGE, AKV * 2 * HD), 1.0, 6.0, ((0, 64), (2, 4))),
        "page_table": draw_page_table(jax.random.fold_in(seeds[13], 71), 0),
        "prefix_pages": draw_prefix_pages(jax.random.fold_in(seeds[13], 71), 0),
        "new_counts": draw_new_counts(jax.random.fold_in(seeds[13], 71), 0),
    }


def pages_to_state(state_pages, heads):
    blocks = state_pages.shape[2] // (2 * HD)
    shaped = state_pages.reshape(SP, PAGE, blocks, 2 * HD).transpose(2, 0, 1, 3)
    return shaped.reshape(heads, HP, NST).astype(jnp.float32)

def scan_block(inner, b_values, c_values, step, rate, skip_gain, state, live):
    length = inner.shape[0]
    heads = step.shape[1]
    values = inner.astype(jnp.float32).reshape(length, heads, HP)
    decay_sum = jnp.cumsum(-step * rate[None, :], axis=0)
    order = jnp.arange(length)
    causal = order[:, None] >= order[None, :]
    gaps = jnp.where(causal[:, :, None], decay_sum[:, None, :] - decay_sum[None, :, :], -jnp.inf)
    intersection = jnp.dot(c_values, b_values.T, preferred_element_type=jnp.float32)
    mixing = jnp.exp(gaps) * intersection[:, :, None] * step[None, :, :]
    local = jnp.einsum('jih,ihp->jhp', mixing, values, precision=lax.Precision.HIGHEST)
    carried = jnp.einsum('hpn,jn->jhp', state, c_values.astype(jnp.float32), precision=lax.Precision.HIGHEST)
    carried = carried * jnp.exp(decay_sum)[:, :, None]
    output = (local + carried + skip_gain[None, :, None] * values) * live[:, None, None]
    return output.reshape(length, heads * HP).astype(jnp.bfloat16)

def attend(queries, fresh, kv_pages, prefix, live):
    length = queries.shape[0]
    kv_heads = fresh.shape[1] // (2 * HD)
    cached = kv_pages.reshape(-1, kv_heads, 2 * HD)
    combined = jnp.concatenate([cached, fresh.reshape(length, kv_heads, 2 * HD)], axis=0)
    keys = combined[:, :, :HD]
    values = combined[:, :, HD:]
    grouped = queries.reshape(length, kv_heads, -1, HD)
    scores = jnp.einsum('jgrd,kgd->grjk', grouped.astype(jnp.float32), keys.astype(jnp.float32), precision=lax.Precision.HIGHEST)
    scores = scores * (1.0 / math.sqrt(HD))
    cached_len = cached.shape[0]
    order = jnp.arange(length)
    slots = jnp.arange(cached_len) // PAGE
    seen = jnp.broadcast_to((slots < prefix)[None, :], (length, cached_len))
    allowed = jnp.concatenate([seen, order[None, :] <= order[:, None]], axis=1)
    scores = jnp.where(allowed[None, None], scores, -jnp.inf)
    top = lax.optimization_barrier(jnp.max(scores, axis=-1, keepdims=True))
    weights = jnp.exp(scores - top)
    weights = (weights / lax.optimization_barrier(jnp.sum(weights, axis=-1, keepdims=True))).astype(jnp.bfloat16)
    mixed = jnp.einsum('grjk,kgd->jgrd', weights.astype(jnp.float32), values.astype(jnp.float32), precision=lax.Precision.HIGHEST)
    mixed = mixed * live[:, None, None, None]
    return mixed.reshape(length, -1).astype(jnp.bfloat16)

def reference(tokens, x_weight, bc_weight, step_weight, step_bias, decay_log, skip_gain, queries, new_keyvals, page_pool, page_table, prefix_pages, new_counts):
    inner = jax.nn.silu(jnp.dot(tokens, x_weight, preferred_element_type=jnp.float32)).astype(jnp.bfloat16)
    column_values = jnp.dot(tokens, bc_weight, preferred_element_type=jnp.float32).astype(jnp.bfloat16)
    step_raw = jnp.dot(tokens, step_weight, preferred_element_type=jnp.float32)
    step_all = jax.nn.softplus(step_raw + step_bias[None, :])
    rate = jnp.exp(decay_log)

    def one_sequence(items):
        inner_seq, column_seq, step_seq, query_seq, fresh_seq, table, prefix, count = items
        order = jnp.arange(NEW)
        live = (order < count).astype(jnp.float32)
        step = step_seq * live[:, None]
        paged = page_pool[table]
        state = pages_to_state(paged[:SP], MH)
        mamba = scan_block(inner_seq, column_seq[:, :NST], column_seq[:, NST:], step, rate, skip_gain, state, live)
        attention = attend(query_seq, fresh_seq, paged[SP:], prefix, live)
        return (mamba, attention)
    mamba_all, attention_all = lax.map(one_sequence, (inner.reshape(SEQS, NEW, -1), column_values.reshape(SEQS, NEW, -1), step_all.reshape(SEQS, NEW, -1), queries.reshape(SEQS, NEW, -1), new_keyvals.reshape(SEQS, NEW, -1), page_table, prefix_pages, new_counts))
    return (mamba_all.reshape(TOKENS, -1), attention_all.reshape(TOKENS, -1))
```

```python
import math

import jax
import jax.numpy as jnp
from jax import lax
from jax.experimental import pallas as pl
from jax.experimental.pallas import tpu as pltpu
from jax.sharding import PartitionSpec as P

HP = 64
NST = 256
HD = 128
PAGE = 128
SP = 16
NY = 4
NZ = 8
NX = 4
VMEM = 48 * 1024 * 1024
ANY = pl.BlockSpec(memory_space=pl.ANY)
WHOLE = pl.BlockSpec(memory_space=pltpu.VMEM)
SCALARS = pl.BlockSpec(memory_space=pltpu.SMEM)


def shift_pairs(axis, by):
    pairs = []
    for y in range(NY):
        for z in range(NZ):
            for core in range(2):
                place = {"y": y, "z": z, "core": core}
                size = {"y": NY, "z": NZ, "core": 2}[axis]
                goal = dict(place)
                goal[axis] = (place[axis] + by) % size
                pairs.append(
                    ((y * NZ + z) * 2 + core, (goal["y"] * NZ + goal["z"]) * 2 + goal["core"])
                )
    return pairs


def move(array, axis, by):
    if axis == "x":
        return lax.ppermute(array, "tensor", [(i, (i + by) % NX) for i in range(NX)])
    return lax.ppermute(array, "dp", shift_pairs(axis, by))


def pack_kernel(picks, pool, out, sems):
    owners = out.shape[0]

    def start(d, carry):
        @pl.when(picks[d] >= 0)
        def _():
            pltpu.make_async_copy(pool.at[picks[d]], out.at[d], sems.at[d]).start()

        return carry

    def finish(d, carry):
        @pl.when(picks[d] >= 0)
        def _():
            pltpu.make_async_copy(pool.at[picks[d]], out.at[d], sems.at[d]).wait()

        return carry

    lax.fori_loop(0, owners, start, 0)
    lax.fori_loop(0, owners, finish, 0)


def pack_pages(picks, pool):
    owners = picks.shape[0]
    page = pool.shape[1:]
    return pl.pallas_call(
        pack_kernel,
        out_shape=jax.ShapeDtypeStruct((owners,) + page, pool.dtype),
        in_specs=[SCALARS, ANY],
        out_specs=ANY,
        scratch_shapes=[pltpu.SemaphoreType.DMA((owners,))],
        cost_estimate=pl.CostEstimate(
            flops=0, bytes_accessed=2 * owners * page[0] * page[1] * 2, transcendentals=0
        ),
        name="pack_pages",
    )(picks, pool)


def project_kernel(count_w, count_t, *refs):
    w_offs, t_rows, t_cols = refs[:3]
    w_pieces = refs[3 : 3 + count_w]
    t_pieces = refs[3 + count_w : 3 + count_w + count_t]
    mine, theirs, mine_extra, theirs_extra, w_all, t_all, sems = refs[3 + count_w + count_t :]
    copies = []
    for i, piece in enumerate(w_pieces):
        rows = piece.shape[0]
        at = pl.multiple_of(w_offs[i], 32)
        copies.append(
            pltpu.make_async_copy(piece, w_all.at[pl.ds(at, rows), :], sems.at[i])
        )
    for i, piece in enumerate(t_pieces):
        rows, cols = piece.shape
        at = pl.multiple_of(t_rows[i], 128)
        along = pl.multiple_of(t_cols[i], 1024)
        copies.append(
            pltpu.make_async_copy(
                piece, t_all.at[pl.ds(at, rows), pl.ds(along, cols)], sems.at[count_w + i]
            )
        )
    for copy in copies:
        copy.start()
    for copy in copies:
        copy.wait()
    half = mine.shape[0]
    wide = 256

    def tile(n, carry):
        at = pl.multiple_of(n * wide, wide)
        total = jnp.dot(
            t_all[...], w_all[:, pl.ds(at, wide)], preferred_element_type=jnp.float32
        )
        value = (total / (1.0 + jnp.exp(-total))).astype(jnp.bfloat16)
        mine[:, pl.ds(at, wide)] = value[:half]
        theirs[:, pl.ds(at, wide)] = value[half:]
        return carry

    main = mine.shape[1]
    lax.fori_loop(0, main // wide, tile, 0)
    extra = jnp.dot(t_all[...], w_all[:, main:], preferred_element_type=jnp.float32)
    mine_extra[...] = extra[:half]
    theirs_extra[...] = extra[half:]


def project(w_pieces, w_offs, t_pieces, t_rows, t_cols, half_rows, main, extra, depth):
    count_w, count_t = len(w_pieces), len(t_pieces)
    return pl.pallas_call(
        lambda *refs: project_kernel(count_w, count_t, *refs),
        out_shape=(
            jax.ShapeDtypeStruct((half_rows, main), jnp.bfloat16),
            jax.ShapeDtypeStruct((half_rows, main), jnp.bfloat16),
            jax.ShapeDtypeStruct((half_rows, extra), jnp.float32),
            jax.ShapeDtypeStruct((half_rows, extra), jnp.float32),
        ),
        in_specs=[SCALARS] * 3 + [ANY] * (count_w + count_t),
        out_specs=(WHOLE,) * 4,
        scratch_shapes=[
            pltpu.VMEM((depth, main + extra), jnp.bfloat16),
            pltpu.VMEM((2 * half_rows, depth), jnp.bfloat16),
            pltpu.SemaphoreType.DMA((count_w + count_t,)),
        ],
        compiler_params=pltpu.CompilerParams(vmem_limit_bytes=VMEM),
        cost_estimate=pl.CostEstimate(
            flops=4 * half_rows * depth * (main + extra),
            bytes_accessed=2 * depth * (main + extra + 2 * half_rows),
            transcendentals=2 * half_rows * main,
        ),
        name="project",
    )(w_offs, t_rows, t_cols, *w_pieces, *t_pieces)


def split_dot(left, right):
    high = left.astype(jnp.bfloat16)
    low = (left - high.astype(jnp.float32)).astype(jnp.bfloat16)
    return jnp.dot(high, right, preferred_element_type=jnp.float32) + jnp.dot(
        low, right, preferred_element_type=jnp.float32
    )


def local_kernel(inner, b_values, c_values, decay, decay_t, step_t, gain, out):
    length = PAGE
    row = lax.broadcasted_iota(jnp.int32, (length, length), 0)
    column = lax.broadcasted_iota(jnp.int32, (length, length), 1)
    causal = row >= column
    first = lax.broadcasted_iota(jnp.int32, (length, 2 * HP), 1) < HP
    for member in range(decay.shape[0]):
        rows = slice(member * length, (member + 1) * length)
        crossing = lax.dot_general(
            c_values[rows, :],
            b_values[rows, :],
            (((1,), (1,)), ((), ())),
            preferred_element_type=jnp.float32,
        )
        for pair in range(decay.shape[2] // 2):
            lanes = slice(pair * 2 * HP, (pair + 1) * 2 * HP)
            values = inner[rows, lanes]
            parts = []
            for head in (2 * pair, 2 * pair + 1):
                gaps = decay[member, :, head : head + 1] - decay_t[member, head : head + 1, :]
                gaps = jnp.where(causal, gaps, -jnp.inf)
                mixing = jnp.exp(gaps) * crossing * step_t[member, head : head + 1, :]
                parts.append(split_dot(mixing, values))
            local = jnp.where(first, parts[0], parts[1])
            out[rows, lanes] = local + gain[:, lanes] * values.astype(jnp.float32)


def mix_locally(inner, b_values, c_values, decay, decay_t, step_t, gain):
    rows, cols = inner.shape
    return pl.pallas_call(
        local_kernel,
        out_shape=jax.ShapeDtypeStruct((rows, cols), jnp.float32),
        in_specs=[WHOLE] * 7,
        out_specs=WHOLE,
        compiler_params=pltpu.CompilerParams(vmem_limit_bytes=VMEM),
        cost_estimate=pl.CostEstimate(
            flops=8 * rows * PAGE * cols, bytes_accessed=6 * rows * cols, transcendentals=rows * PAGE * 32
        ),
        name="mix_locally",
    )(inner, b_values, c_values, decay, decay_t, step_t, gain)


def carry_kernel(sources, incoming, c_values, decay, live, local, out, held, sems):
    members, pages = decay.shape[0], SP

    def copy(member, page):
        return pltpu.make_async_copy(
            incoming.at[sources[member, page]],
            held.at[member * pages + page],
            sems.at[member * pages + page],
        )

    for member in range(members):
        for page in range(pages):
            copy(member, page).start()
    first = lax.broadcasted_iota(jnp.int32, (PAGE, 2 * HP), 1) < HP
    for member in range(members):
        rows = slice(member * PAGE, (member + 1) * PAGE)
        fade = jnp.exp(decay[member])
        for page in range(pages):
            lanes = slice(page * 2 * HP, (page + 1) * 2 * HP)
            copy(member, page).wait()
            carried = lax.dot_general(
                c_values[rows, :],
                held[member * pages + page],
                (((1,), (1,)), ((), ())),
                preferred_element_type=jnp.float32,
            )
            factor = jnp.where(
                first, fade[:, 2 * page : 2 * page + 1], fade[:, 2 * page + 1 : 2 * page + 2]
            )
            total = (local[rows, lanes] + carried * factor) * live[rows, :]
            out[rows, lanes] = total.astype(jnp.bfloat16)


def carry_state(sources, incoming, c_values, decay, live, local):
    rows, cols = local.shape
    members = decay.shape[0]
    return pl.pallas_call(
        carry_kernel,
        out_shape=jax.ShapeDtypeStruct((rows, cols), jnp.bfloat16),
        in_specs=[SCALARS, ANY] + [WHOLE] * 4,
        out_specs=WHOLE,
        scratch_shapes=[
            pltpu.VMEM((members * SP,) + incoming.shape[1:], incoming.dtype),
            pltpu.SemaphoreType.DMA((members * SP,)),
        ],
        compiler_params=pltpu.CompilerParams(vmem_limit_bytes=VMEM),
        cost_estimate=pl.CostEstimate(
            flops=2 * rows * NST * cols, bytes_accessed=8 * rows * cols, transcendentals=0
        ),
        name="carry_state",
    )(sources, incoming, c_values, decay, live, local)


CHUNK = 8


def attend_kernel(sources, prefix, queries, fresh, live, incoming, out, stacked, held, top, total, sems):
    members, slots = sources.shape
    heads = queries.shape[1] // HD
    factor = math.log2(math.e) / math.sqrt(HD)
    nothing = -1e30

    def copy(member, slot):
        return pltpu.make_async_copy(
            incoming.at[sources[member, slot]],
            held.at[member, pl.ds(pl.multiple_of(slot * PAGE, PAGE), PAGE), :],
            sems.at[member, slot],
        )

    for member in range(members):

        def start(slot, carry):
            @pl.when(slot < prefix[member])
            def _():
                copy(member, slot).start()

            @pl.when(slot >= prefix[member])
            def _():
                held[member, pl.ds(pl.multiple_of(slot * PAGE, PAGE), PAGE), :] = jnp.zeros(
                    (PAGE, 2 * HD), held.dtype
                )

            return carry

        lax.fori_loop(0, slots, start, 0)

    wide = CHUNK * PAGE
    block = 2 * PAGE
    causal = lax.broadcasted_iota(jnp.int32, (block, PAGE), 0) % PAGE >= lax.broadcasted_iota(
        jnp.int32, (block, PAGE), 1
    )
    for member in range(members):
        rows = slice(member * PAGE, (member + 1) * PAGE)
        for head in range(heads):
            stacked[head * PAGE : (head + 1) * PAGE, :] = queries[rows, head * HD : (head + 1) * HD]
        new_keys = fresh[rows, :HD]
        new_values = jnp.concatenate([jnp.ones((PAGE, HD), jnp.bfloat16), fresh[rows, HD:]], axis=1)
        for part in range(heads // 2):
            at = slice(part * block, (part + 1) * block)
            scores = lax.dot_general(
                stacked[at, :], new_keys, (((1,), (1,)), ((), ())), preferred_element_type=jnp.float32
            )
            scores = jnp.where(causal, scores * factor, nothing)
            best = jnp.max(scores, axis=1, keepdims=True)
            weights = jnp.exp2(scores - best).astype(jnp.bfloat16)
            top[at, :] = jnp.broadcast_to(best, (block, HD))
            total[at, :] = jnp.dot(weights, new_values, preferred_element_type=jnp.float32)

        def chunk(index, carry):
            base = index * CHUNK

            def finish(slot, inside):
                @pl.when(base + slot < prefix[member])
                def _():
                    copy(member, base + slot).wait()

                return inside

            lax.fori_loop(0, CHUNK, finish, 0)
            span = pl.ds(pl.multiple_of(index * wide, wide), wide)
            keys = held[member, span, :HD]
            values = jnp.concatenate([jnp.ones((wide, HD), jnp.bfloat16), held[member, span, HD:]], axis=1)
            seen = index * wide + lax.broadcasted_iota(jnp.int32, (1, wide), 1) < prefix[member] * PAGE
            bias = jnp.where(seen, 0.0, nothing)
            for part in range(heads // 2):
                at = slice(part * block, (part + 1) * block)
                scores = lax.dot_general(
                    stacked[at, :], keys, (((1,), (1,)), ((), ())), preferred_element_type=jnp.float32
                )
                scores = scores * factor + bias
                before = top[at, :1]
                best = jnp.maximum(before, jnp.max(scores, axis=1, keepdims=True))
                weights = jnp.exp2(scores - best).astype(jnp.bfloat16)
                shrink = jnp.exp2(before - best)
                top[at, :] = jnp.broadcast_to(best, (block, HD))
                total[at, :] = total[at, :] * shrink + jnp.dot(
                    weights, values, preferred_element_type=jnp.float32
                )
            return carry

        lax.fori_loop(0, (prefix[member] + CHUNK - 1) // CHUNK, chunk, 0)
        for head in range(heads):
            at = slice(head * PAGE, (head + 1) * PAGE)
            mixed = total[at, HD:] / total[at, :HD] * live[rows, :]
            out[rows, head * HD : (head + 1) * HD] = mixed.astype(jnp.bfloat16)


def attend(sources, prefix, queries, fresh, live, incoming):
    rows, cols = queries.shape
    members, slots = sources.shape
    heads = cols // HD
    return pl.pallas_call(
        attend_kernel,
        out_shape=jax.ShapeDtypeStruct((rows, cols), jnp.bfloat16),
        in_specs=[SCALARS, SCALARS] + [WHOLE] * 3 + [ANY],
        out_specs=WHOLE,
        scratch_shapes=[
            pltpu.VMEM((heads * PAGE, HD), jnp.bfloat16),
            pltpu.VMEM((members, slots * PAGE, 2 * HD), jnp.bfloat16),
            pltpu.VMEM((heads * PAGE, HD), jnp.float32),
            pltpu.VMEM((heads * PAGE, 2 * HD), jnp.float32),
            pltpu.SemaphoreType.DMA((members, slots)),
        ],
        compiler_params=pltpu.CompilerParams(vmem_limit_bytes=VMEM),
        cost_estimate=pl.CostEstimate(
            flops=4 * rows * cols * slots * PAGE,
            bytes_accessed=members * slots * PAGE * 4 * HD,
            transcendentals=rows * heads * slots * PAGE,
        ),
        name="attend",
    )(sources, prefix, queries, fresh, live, incoming)


def gather_weights(block, y, z):
    rows = block.shape[0]
    half = rows // 2

    def first_row(along_y, along_z):
        return (((y + along_y) % NY) * NZ + (z + along_z) % NZ) * rows

    ring = [(block, 0, 0)]
    up = down = block
    for hop in range(1, NZ // 2):
        up, down = move(up, "z", 1), move(down, "z", -1)
        ring += [(up, -hop, 0), (down, hop, 0)]
    far = NZ // 2
    ring += [(move(up[:half], "z", 1), far, 0), (move(down[half:], "z", -1), far, half)]
    pieces, offsets = [], []
    for piece, along, inside in ring:
        middle = piece.shape[0] // 2
        up, down = move(piece, "y", 1), move(piece, "y", -1)
        pieces += [piece, up, down, move(up[:middle], "y", 1), move(down[middle:], "y", -1)]
        offsets += [
            first_row(0, along) + inside,
            first_row(-1, along) + inside,
            first_row(1, along) + inside,
            first_row(2, along) + inside,
            first_row(2, along) + inside + middle,
        ]
    return pieces, offsets


def gather_tokens(tokens, x):
    rows, cols = tokens.shape
    middle = rows // 2
    up, down = move(tokens, "x", 1), move(tokens, "x", -1)
    own = [
        (tokens, 0, x),
        (up, 0, (x - 1) % NX),
        (down, 0, (x + 1) % NX),
        (move(up[:middle], "x", 1), 0, (x + 2) % NX),
        (move(down[middle:], "x", -1), middle, (x + 2) % NX),
    ]
    partner = [(move(piece, "core", 1), rows + at, block) for piece, at, block in own]
    every = own + partner
    return [e[0] for e in every], [e[1] for e in every], [e[2] * cols for e in every]


def body(
    tokens,
    x_weight,
    bc_weight,
    step_weight,
    step_bias,
    decay_log,
    skip_gain,
    queries,
    new_keyvals,
    page_pool,
    page_table,
    prefix_pages,
    new_counts,
):
    owners = lax.axis_size("dp")
    position = lax.axis_index("dp")
    x = lax.axis_index("tensor")
    core = position % 2
    z = (position // 2) % NZ
    y = position // (2 * NZ)
    seq_dev = page_table.shape[0]
    pool_size = page_pool.shape[0]
    rows = tokens.shape[0]
    length = rows // seq_dev
    heads = step_bias.shape[0]

    sources = page_table // pool_size
    places = page_table % pool_size
    names = jnp.arange(owners, dtype=jnp.int32)[:, None]

    def wanted(part):
        asked = sources[:, part].reshape(1, -1) == names
        return jnp.max(jnp.where(asked, places[:, part].reshape(1, -1), -1), axis=1)

    asks = jnp.stack([wanted(slice(SP, None)), wanted(slice(0, SP))], axis=1)
    asks = jnp.pad(asks, ((0, 0), (0, 126))).reshape(owners, 1, 128)
    picks = lax.all_to_all(asks, "dp", split_axis=0, concat_axis=0, tiled=True)
    kv_out = pack_pages(picks[:, 0, 0], page_pool)
    kv_in = lax.all_to_all(kv_out, "dp", split_axis=0, concat_axis=0, tiled=True)
    state_out = pack_pages(picks[:, 0, 1], page_pool)
    state_in = lax.all_to_all(state_out, "dp", split_axis=0, concat_axis=0, tiled=True)

    main = x_weight.shape[1] // 2
    extra = bc_weight.shape[1]
    step_wide = jnp.pad(step_weight, ((0, 0), (0, extra - heads)))
    low = jnp.concatenate([x_weight[:, :main], bc_weight], axis=1)
    high = jnp.concatenate([x_weight[:, main:], step_wide], axis=1)
    own = jnp.where(core == 0, low, high)
    other = move(jnp.where(core == 0, high, low), "core", 1)
    block = jnp.where(
        core == 0, jnp.concatenate([own, other], axis=0), jnp.concatenate([other, own], axis=0)
    )
    w_pieces, w_offs = gather_weights(block, y, z)
    t_pieces, t_rows, t_cols = gather_tokens(tokens, x)
    mine, theirs, mine_extra, theirs_extra = project(
        w_pieces,
        jnp.stack(w_offs).astype(jnp.int32),
        t_pieces,
        jnp.array(t_rows, jnp.int32),
        jnp.stack(t_cols).astype(jnp.int32),
        rows,
        main,
        extra,
        owners * x_weight.shape[0],
    )
    got, got_extra = move(theirs, "core", 1), move(theirs_extra, "core", 1)
    inner = jnp.where(
        core == 0, jnp.concatenate([mine, got], axis=1), jnp.concatenate([got, mine], axis=1)
    )
    columns = jnp.where(core == 0, mine_extra, got_extra).astype(jnp.bfloat16)
    step_raw = jnp.where(core == 0, got_extra, mine_extra)[:, :heads]
    around = jnp.stack([columns] + [move(columns, "x", -k) for k in range(1, NX)])
    quarters = [lax.dynamic_index_in_dim(around, (t - x) % NX, 0, keepdims=False) for t in range(NX)]
    b_values = jnp.concatenate(quarters[:2], axis=1)
    c_values = jnp.concatenate(quarters[2:], axis=1)

    live = (jnp.arange(length)[None, :] < new_counts[:, None]).astype(jnp.float32)
    step = jax.nn.softplus(step_raw + step_bias[None, :]).reshape(seq_dev, length, heads)
    step = step * live[:, :, None]
    decay = jnp.cumsum(-step * jnp.exp(decay_log)[None, None, :], axis=1)
    gain = jnp.repeat(skip_gain, HP)[None, :]
    live_column = live.reshape(rows, 1)
    local = mix_locally(
        inner, b_values, c_values, decay, decay.transpose(0, 2, 1), step.transpose(0, 2, 1), gain
    )
    attention_out = attend(
        sources[:, SP:], prefix_pages, queries, new_keyvals, live_column, kv_in
    )
    mamba_out = carry_state(sources[:, :SP], state_in, c_values, decay, live_column, local)
    return (mamba_out, attention_out)


def solution(mesh):
    placed = (
        P("dp", "tensor"),
        P("dp", "tensor"),
        P("dp", "tensor"),
        P("dp", "tensor"),
        P("tensor"),
        P("tensor"),
        P("tensor"),
        P("dp", "tensor"),
        P("dp", "tensor"),
        P("dp", None, "tensor"),
        P("dp", None),
        P("dp"),
        P("dp"),
    )
    return jax.shard_map(
        body,
        mesh=mesh,
        in_specs=placed,
        out_specs=(P("dp", "tensor"), P("dp", "tensor")),
        check_vma=False,
    )
```

```python
import functools
import math

import jax
import jax.numpy as jnp
from jax import lax
from jax.experimental import pallas as pl
from jax.experimental.pallas import tpu as pltpu
from jax.sharding import Mesh
from jax.sharding import PartitionSpec as P

HP = 64
NST = 256
HD = 128
PAGE = 128
SP = 16
NY = 4
NZ = 8
NX = 4
DP = ("y", "z", "core")
VMEM = 48 * 1024 * 1024
ANY = pl.BlockSpec(memory_space=pl.ANY)
HBM = pl.BlockSpec(memory_space=pltpu.HBM)
WHOLE = pl.BlockSpec(memory_space=pltpu.VMEM)
SCALARS = pl.BlockSpec(memory_space=pltpu.SMEM)


def around_x(array, by):
    return lax.ppermute(array, "tensor", [(i, (i + by) % NX) for i in range(NX)])


def pack_kernel(column, picks, pool, out, held, in_sems, out_sems):
    owners = out.shape[0]
    parts = in_sems.shape[0]
    span = owners // parts

    def fetch(r, part):
        pltpu.make_async_copy(pool.at[picks[r, 0, column]], held.at[r], in_sems.at[part]).start()
        return part

    def store(part):
        rows = pl.ds(part * span, span)
        return pltpu.make_async_copy(held.at[rows], out.at[rows], out_sems.at[part])

    for part in range(parts):
        lax.fori_loop(part * span, (part + 1) * span, fetch, part, unroll=8)
    for part in range(parts):
        rows = pl.ds(part * span, span)
        pltpu.make_async_copy(pool.at[pl.ds(0, span)], held.at[rows], in_sems.at[part]).wait()
        store(part).start()
    for part in range(parts):
        store(part).wait()


def pack_pages(picks, column, pool):
    owners = picks.shape[0]
    page = pool.shape[1:]
    return pl.pallas_call(
        functools.partial(pack_kernel, column),
        out_shape=jax.ShapeDtypeStruct((owners,) + page, pool.dtype),
        in_specs=[SCALARS, HBM],
        out_specs=HBM,
        scratch_shapes=[
            pltpu.VMEM((owners,) + page, pool.dtype),
            pltpu.SemaphoreType.DMA((4,)),
            pltpu.SemaphoreType.DMA((4,)),
        ],
        compiler_params=pltpu.CompilerParams(vmem_limit_bytes=62 * 1024 * 1024),
        cost_estimate=pl.CostEstimate(
            flops=0, bytes_accessed=4 * owners * page[0] * page[1], transcendentals=0
        ),
        name="pack_pages",
    )(picks, pool)


def project_kernel(x, weights, *refs):
    pieces = refs[:5]
    main_out, extra_out, w_all, t_all, w_sems, t_sems = refs[5:]
    tiles, wide = w_all.shape[0], w_all.shape[5]
    depth = t_all.shape[1]
    cols = pieces[0].shape[1]
    middle = pieces[3].shape[0]

    def columns(n):
        along = pl.ds(pl.multiple_of(n * wide, wide), wide)
        return [
            pltpu.make_async_copy(
                weights.at[y, core, :, :, along], w_all.at[n, y, :, core], w_sems.at[n, 2 * y + core]
            )
            for y in range(NY)
            for core in range(2)
        ]

    def start(n, carry):
        for copy in columns(n):
            copy.start()
        return carry

    copies = []
    for i, (first, by) in enumerate(((0, 0), (0, NX - 1), (0, 1), (0, 2), (middle, 2))):
        along = pl.multiple_of((x[0] + by) % NX * cols, cols)
        rows = pieces[i].shape[0]
        copies.append(
            pltpu.make_async_copy(
                pieces[i], t_all.at[pl.ds(first, rows), pl.ds(along, cols)], t_sems.at[i]
            )
        )
    for copy in copies:
        copy.start()
    lax.fori_loop(0, tiles, start, 0)
    for copy in copies:
        copy.wait()

    def product(n):
        for copy in columns(n):
            copy.wait()
        tile = w_all[n].reshape(depth, wide)
        return jnp.dot(t_all[...], tile, preferred_element_type=jnp.float32)

    def main_tile(n, carry):
        total = product(n)
        value = total / (1.0 + jnp.exp(-total))
        main_out[:, pl.ds(pl.multiple_of(n * wide, wide), wide)] = value.astype(jnp.bfloat16)
        return carry

    lax.fori_loop(0, tiles - 1, main_tile, 0)
    extra_out[...] = product(tiles - 1)


def project(x, weights, pieces, rows, wide):
    cols = weights.shape[-1]
    depth = weights.size // cols
    main = cols - wide
    return pl.pallas_call(
        project_kernel,
        out_shape=(
            jax.ShapeDtypeStruct((rows, main), jnp.bfloat16),
            jax.ShapeDtypeStruct((rows, wide), jnp.float32),
        ),
        in_specs=[SCALARS, HBM] + [ANY] * 5,
        out_specs=(WHOLE,) * 2,
        scratch_shapes=[
            pltpu.VMEM((cols // wide, NY, NZ, 2, depth // (2 * NY * NZ), wide), jnp.bfloat16),
            pltpu.VMEM((rows, depth), jnp.bfloat16),
            pltpu.SemaphoreType.DMA((cols // wide, 2 * NY)),
            pltpu.SemaphoreType.DMA((5,)),
        ],
        compiler_params=pltpu.CompilerParams(vmem_limit_bytes=VMEM),
        cost_estimate=pl.CostEstimate(
            flops=2 * rows * depth * cols, bytes_accessed=2 * depth * (cols + rows), transcendentals=rows * main
        ),
        name="project",
    )(x, weights, *pieces)


def split_dot(left, right):
    high = left.astype(jnp.bfloat16)
    low = (left - high.astype(jnp.float32)).astype(jnp.bfloat16)
    return jnp.dot(high, right, preferred_element_type=jnp.float32) + jnp.dot(
        low, right, preferred_element_type=jnp.float32
    )


def local_kernel(inner, b_values, c_values, decay, decay_t, step_t, gain, live, out, factor):
    length = PAGE
    row = lax.broadcasted_iota(jnp.int32, (length, length), 0)
    column = lax.broadcasted_iota(jnp.int32, (length, length), 1)
    causal = row >= column
    first = lax.broadcasted_iota(jnp.int32, (length, 2 * HP), 1) < HP
    for member in range(decay.shape[0]):
        rows = slice(member * length, (member + 1) * length)
        crossing = lax.dot_general(
            c_values[rows, :],
            b_values[rows, :],
            (((1,), (1,)), ((), ())),
            preferred_element_type=jnp.float32,
        )
        fades = jnp.exp(decay[member])
        for pair in range(decay.shape[2] // 2):
            lanes = slice(pair * 2 * HP, (pair + 1) * 2 * HP)
            values = inner[rows, lanes]
            parts = []
            for head in (2 * pair, 2 * pair + 1):
                gaps = decay[member, :, head : head + 1] - decay_t[member, head : head + 1, :]
                gaps = jnp.where(causal, gaps, -jnp.inf)
                mixing = jnp.exp(gaps) * crossing * step_t[member, head : head + 1, :]
                parts.append(split_dot(mixing, values))
            local = jnp.where(first, parts[0], parts[1])
            local = local + gain[:, lanes] * values.astype(jnp.float32)
            out[rows, lanes] = local * live[rows, :]
            fade = jnp.where(first, fades[:, 2 * pair : 2 * pair + 1], fades[:, 2 * pair + 1 : 2 * pair + 2])
            factor[rows, lanes] = fade * live[rows, :]


def mix_locally(inner, b_values, c_values, decay, decay_t, step_t, gain, live):
    rows, cols = inner.shape
    return pl.pallas_call(
        local_kernel,
        out_shape=(jax.ShapeDtypeStruct((rows, cols), jnp.float32),) * 2,
        in_specs=[WHOLE] * 8,
        out_specs=(WHOLE,) * 2,
        compiler_params=pltpu.CompilerParams(vmem_limit_bytes=VMEM),
        cost_estimate=pl.CostEstimate(
            flops=8 * rows * PAGE * cols, bytes_accessed=6 * rows * cols, transcendentals=rows * PAGE * 32
        ),
        name="mix_locally",
    )(inner, b_values, c_values, decay, decay_t, step_t, gain, live)


def carry_kernel(
    sources, incoming, c_values, factor, local, out, held, factors, locals_, ready, in_sems, out_sems
):
    members = sources.shape[0]
    span = 2 * PAGE

    def rows_of(member):
        return pl.ds(member * PAGE, PAGE)

    def bring(member):
        rows = rows_of(member)
        return [
            pltpu.make_async_copy(factor.at[rows, :], factors.at[rows, :], in_sems.at[member, 1]),
            pltpu.make_async_copy(local.at[rows, :], locals_.at[rows, :], in_sems.at[member, 2]),
        ]

    def store(member):
        rows = rows_of(member)
        return pltpu.make_async_copy(ready.at[rows, :], out.at[rows, :], out_sems.at[member])

    for member in range(members):
        for page in range(SP):
            pltpu.make_async_copy(
                incoming.at[sources[member, page]], held.at[member * SP + page], in_sems.at[member, 0]
            ).start()
        for copy in bring(member):
            copy.start()
    for member in range(members):
        rows = rows_of(member)
        pages = pl.ds(member * SP, SP)
        pltpu.make_async_copy(incoming.at[pl.ds(0, SP)], held.at[pages], in_sems.at[member, 0]).wait()
        for copy in bring(member):
            copy.wait()
        for page in range(0, SP, 2):
            lanes = slice(page * 2 * HP, page * 2 * HP + span)
            pair = held[member * SP + page : member * SP + page + 2].reshape(span, NST)
            carried = lax.dot_general(
                c_values[rows, :], pair, (((1,), (1,)), ((), ())), preferred_element_type=jnp.float32
            )
            total = locals_[rows, lanes] + carried * factors[rows, lanes]
            ready[rows, lanes] = total.astype(jnp.bfloat16)
        store(member).start()
    for member in range(members):
        store(member).wait()


def carry_state(sources, incoming, c_values, factor, local):
    rows, cols = local.shape
    members = sources.shape[0]
    return pl.pallas_call(
        carry_kernel,
        out_shape=jax.ShapeDtypeStruct((rows, cols), jnp.bfloat16),
        in_specs=[SCALARS, HBM, WHOLE, HBM, HBM],
        out_specs=HBM,
        scratch_shapes=[
            pltpu.VMEM((members * SP,) + incoming.shape[1:], incoming.dtype),
            pltpu.VMEM((rows, cols), jnp.float32),
            pltpu.VMEM((rows, cols), jnp.float32),
            pltpu.VMEM((rows, cols), jnp.bfloat16),
            pltpu.SemaphoreType.DMA((members, 3)),
            pltpu.SemaphoreType.DMA((members,)),
        ],
        compiler_params=pltpu.CompilerParams(vmem_limit_bytes=VMEM),
        cost_estimate=pl.CostEstimate(
            flops=2 * rows * NST * cols, bytes_accessed=8 * rows * cols, transcendentals=0
        ),
        name="carry_state",
    )(sources, incoming, c_values, factor, local)


CHUNK = 8


def attend_kernel(sources, prefix, queries, fresh, live, incoming, out, stacked, held, top, total, sems):
    members, slots = sources.shape
    heads = queries.shape[1] // HD
    factor = math.log2(math.e) / math.sqrt(HD)
    nothing = -1e30

    def copy(member, slot):
        return pltpu.make_async_copy(
            incoming.at[sources[member, slot]],
            held.at[member, pl.ds(pl.multiple_of(slot * PAGE, PAGE), PAGE), :],
            sems.at[member, slot],
        )

    for member in range(members):

        def start(slot, carry):
            @pl.when(slot < prefix[member])
            def _():
                copy(member, slot).start()

            @pl.when(slot >= prefix[member])
            def _():
                held[member, pl.ds(pl.multiple_of(slot * PAGE, PAGE), PAGE), :] = jnp.zeros(
                    (PAGE, 2 * HD), held.dtype
                )

            return carry

        lax.fori_loop(0, slots, start, 0)

    wide = CHUNK * PAGE
    block = 2 * PAGE
    causal = lax.broadcasted_iota(jnp.int32, (block, PAGE), 0) % PAGE >= lax.broadcasted_iota(
        jnp.int32, (block, PAGE), 1
    )
    for member in range(members):
        rows = slice(member * PAGE, (member + 1) * PAGE)
        for head in range(heads):
            stacked[head * PAGE : (head + 1) * PAGE, :] = queries[rows, head * HD : (head + 1) * HD]
        new_keys = fresh[rows, :HD]
        new_values = jnp.concatenate([jnp.ones((PAGE, HD), jnp.bfloat16), fresh[rows, HD:]], axis=1)
        for part in range(heads // 2):
            at = slice(part * block, (part + 1) * block)
            scores = lax.dot_general(
                stacked[at, :], new_keys, (((1,), (1,)), ((), ())), preferred_element_type=jnp.float32
            )
            scores = jnp.where(causal, scores * factor, nothing)
            best = jnp.max(scores, axis=1, keepdims=True)
            weights = jnp.exp2(scores - best).astype(jnp.bfloat16)
            top[at, :] = jnp.broadcast_to(best, (block, HD))
            total[at, :] = jnp.dot(weights, new_values, preferred_element_type=jnp.float32)

        def chunk(index, carry):
            base = index * CHUNK

            def finish(slot, inside):
                @pl.when(base + slot < prefix[member])
                def _():
                    copy(member, base + slot).wait()

                return inside

            lax.fori_loop(0, CHUNK, finish, 0)
            span = pl.ds(pl.multiple_of(index * wide, wide), wide)
            keys = held[member, span, :HD]
            values = jnp.concatenate([jnp.ones((wide, HD), jnp.bfloat16), held[member, span, HD:]], axis=1)
            seen = index * wide + lax.broadcasted_iota(jnp.int32, (1, wide), 1) < prefix[member] * PAGE
            bias = jnp.where(seen, 0.0, nothing)
            for part in range(heads // 2):
                at = slice(part * block, (part + 1) * block)
                scores = lax.dot_general(
                    stacked[at, :], keys, (((1,), (1,)), ((), ())), preferred_element_type=jnp.float32
                )
                scores = scores * factor + bias
                before = top[at, :1]
                best = jnp.maximum(before, jnp.max(scores, axis=1, keepdims=True))
                weights = jnp.exp2(scores - best).astype(jnp.bfloat16)
                shrink = jnp.exp2(before - best)
                top[at, :] = jnp.broadcast_to(best, (block, HD))
                total[at, :] = total[at, :] * shrink + jnp.dot(
                    weights, values, preferred_element_type=jnp.float32
                )
            return carry

        lax.fori_loop(0, (prefix[member] + CHUNK - 1) // CHUNK, chunk, 0)
        for head in range(heads):
            at = slice(head * PAGE, (head + 1) * PAGE)
            mixed = total[at, HD:] / total[at, :HD] * live[rows, :]
            out[rows, head * HD : (head + 1) * HD] = mixed.astype(jnp.bfloat16)


def attend(sources, prefix, queries, fresh, live, incoming):
    rows, cols = queries.shape
    members, slots = sources.shape
    heads = cols // HD
    return pl.pallas_call(
        attend_kernel,
        out_shape=jax.ShapeDtypeStruct((rows, cols), jnp.bfloat16),
        in_specs=[SCALARS, SCALARS] + [WHOLE] * 3 + [HBM],
        out_specs=WHOLE,
        scratch_shapes=[
            pltpu.VMEM((heads * PAGE, HD), jnp.bfloat16),
            pltpu.VMEM((members, slots * PAGE, 2 * HD), jnp.bfloat16),
            pltpu.VMEM((heads * PAGE, HD), jnp.float32),
            pltpu.VMEM((heads * PAGE, 2 * HD), jnp.float32),
            pltpu.SemaphoreType.DMA((members, slots)),
        ],
        compiler_params=pltpu.CompilerParams(vmem_limit_bytes=VMEM),
        cost_estimate=pl.CostEstimate(
            flops=4 * rows * cols * slots * PAGE,
            bytes_accessed=members * slots * PAGE * 4 * HD,
            transcendentals=rows * heads * slots * PAGE,
        ),
        name="attend",
    )(sources, prefix, queries, fresh, live, incoming)


def gather_tokens(tokens):
    middle = tokens.shape[0] // 2
    up, down = around_x(tokens, 1), around_x(tokens, -1)
    return [tokens, up, down, around_x(up[:middle], 1), around_x(down[middle:], -1)]


def body(
    tokens,
    x_weight,
    bc_weight,
    step_weight,
    step_bias,
    decay_log,
    skip_gain,
    queries,
    new_keyvals,
    page_pool,
    page_table,
    prefix_pages,
    new_counts,
):
    owners = lax.axis_size(DP)
    x = lax.axis_index("tensor")
    seq_dev = page_table.shape[0]
    pool_size = page_pool.shape[0]
    rows = tokens.shape[0]
    length = rows // seq_dev
    heads = step_bias.shape[0]

    sources = page_table // pool_size
    places = page_table % pool_size
    names = jnp.arange(owners, dtype=jnp.int32)[:, None]

    def wanted(part):
        asked = sources[:, part].reshape(1, -1) == names
        return jnp.max(jnp.where(asked, places[:, part].reshape(1, -1), 0), axis=1)

    asks = jnp.stack([wanted(slice(SP, None)), wanted(slice(0, SP))], axis=1)
    asks = jnp.pad(asks, ((0, 0), (0, 126))).reshape(owners, 1, 128)
    extra = bc_weight.shape[1]
    x_weight, bc_weight, step_weight, asks = lax.optimization_barrier(
        (x_weight, bc_weight, step_weight, asks)
    )
    step_wide = jnp.pad(step_weight, ((0, 0), (0, extra - heads)))
    weights = jnp.concatenate([x_weight, bc_weight, step_wide], axis=1)
    weights = lax.all_gather(weights, "z", axis=0)
    picks = lax.all_to_all(asks, DP, split_axis=0, concat_axis=0, tiled=True)
    kv_out = pack_pages(picks, 0, page_pool)
    kv_in = lax.all_to_all(kv_out, DP, split_axis=0, concat_axis=0, tiled=True)
    state_out = pack_pages(picks, 1, page_pool)
    state_in = lax.all_to_all(state_out, DP, split_axis=0, concat_axis=0, tiled=True)

    weights, _ = lax.optimization_barrier((weights, state_out))
    weights = lax.all_gather(weights, ("y", "core"), axis=0)
    weights = weights.reshape((NY, 2) + weights.shape[1:])
    tokens, _ = lax.optimization_barrier((tokens, kv_out))
    inner, extras = project(
        x.reshape(1).astype(jnp.int32), weights, gather_tokens(tokens), rows, 2 * extra
    )
    columns = extras[:, :extra].astype(jnp.bfloat16)
    step_raw = extras[:, extra : extra + heads]
    around = jnp.stack([columns] + [around_x(columns, -k) for k in range(1, NX)])
    quarters = [lax.dynamic_index_in_dim(around, (t - x) % NX, 0, keepdims=False) for t in range(NX)]
    b_values = jnp.concatenate(quarters[:2], axis=1)
    c_values = jnp.concatenate(quarters[2:], axis=1)

    live = (jnp.arange(length)[None, :] < new_counts[:, None]).astype(jnp.float32)
    step = jax.nn.softplus(step_raw + step_bias[None, :]).reshape(seq_dev, length, heads)
    step = step * live[:, :, None]
    decay = jnp.cumsum(-step * jnp.exp(decay_log)[None, None, :], axis=1)
    gain = jnp.repeat(skip_gain, HP)[None, :]
    live_column = live.reshape(rows, 1)
    local, factor = mix_locally(
        inner, b_values, c_values, decay, decay.transpose(0, 2, 1), step.transpose(0, 2, 1), gain, live_column
    )
    attention_out = attend(
        sources[:, SP:], prefix_pages, queries, new_keyvals, live_column, kv_in
    )
    mamba_out = carry_state(sources[:, :SP], state_in, c_values, factor, local)
    return (mamba_out, attention_out)


def solution(mesh):
    split = Mesh(mesh.devices.reshape(NY, NZ, 2, NX), DP + ("tensor",))
    placed = (
        P(DP, "tensor"),
        P(DP, "tensor"),
        P(DP, "tensor"),
        P(DP, "tensor"),
        P("tensor"),
        P("tensor"),
        P("tensor"),
        P(DP, "tensor"),
        P(DP, "tensor"),
        P(DP, None, "tensor"),
        P(DP, None),
        P(DP),
        P(DP),
    )
    return jax.shard_map(
        body,
        mesh=split,
        in_specs=placed,
        out_specs=(P(DP, "tensor"), P(DP, "tensor")),
        check_vma=False,
    )
```

```python
import functools
import math

import jax
import jax.numpy as jnp
from jax import lax
from jax.experimental import pallas as pl
from jax.experimental.pallas import tpu as pltpu
from jax.sharding import Mesh
from jax.sharding import PartitionSpec as P

HP = 64
NST = 256
HD = 128
PAGE = 128
SP = 16
NY = 4
NZ = 8
NX = 4
DP = ("y", "z", "core")
VMEM = 62 * 1024 * 1024
ANY = pl.BlockSpec(memory_space=pl.ANY)
HBM = pl.BlockSpec(memory_space=pltpu.HBM)
WHOLE = pl.BlockSpec(memory_space=pltpu.VMEM)
SCALARS = pl.BlockSpec(memory_space=pltpu.SMEM)


def around_x(array, by):
    return lax.ppermute(array, "tensor", [(i, (i + by) % NX) for i in range(NX)])


def pack_kernel(column, picks, pool, out, held, in_sems, out_sems):
    owners = out.shape[0]
    parts = in_sems.shape[0]
    span = owners // parts

    def fetch(r, part):
        pltpu.make_async_copy(pool.at[picks[r, 0, column]], held.at[r], in_sems.at[part]).start()
        return part

    def store(part):
        rows = pl.ds(part * span, span)
        return pltpu.make_async_copy(held.at[rows], out.at[rows], out_sems.at[part])

    for part in range(parts):
        lax.fori_loop(part * span, (part + 1) * span, fetch, part, unroll=8)
    for part in range(parts):
        rows = pl.ds(part * span, span)
        pltpu.make_async_copy(pool.at[pl.ds(0, span)], held.at[rows], in_sems.at[part]).wait()
        store(part).start()
    for part in range(parts):
        store(part).wait()


def pack_pages(picks, column, pool):
    owners = picks.shape[0]
    page = pool.shape[1:]
    return pl.pallas_call(
        functools.partial(pack_kernel, column),
        out_shape=jax.ShapeDtypeStruct((owners,) + page, pool.dtype),
        in_specs=[SCALARS, HBM],
        out_specs=HBM,
        scratch_shapes=[
            pltpu.VMEM((owners,) + page, pool.dtype),
            pltpu.SemaphoreType.DMA((4,)),
            pltpu.SemaphoreType.DMA((4,)),
        ],
        compiler_params=pltpu.CompilerParams(vmem_limit_bytes=VMEM),
        cost_estimate=pl.CostEstimate(
            flops=0, bytes_accessed=4 * owners * page[0] * page[1], transcendentals=0
        ),
        name="pack_pages",
    )(picks, pool)


def project_kernel(x, weights, *refs):
    pieces = refs[:5]
    main_out, extra_out, w_all, t_all, w_sems, t_sems = refs[5:]
    tiles, wide = w_all.shape[0], w_all.shape[5]
    depth = t_all.shape[1]
    cols = pieces[0].shape[1]
    middle = pieces[3].shape[0]

    def columns(n):
        along = pl.ds(pl.multiple_of(n * wide, wide), wide)
        return [
            pltpu.make_async_copy(
                weights.at[y, core, :, :, along], w_all.at[n, y, :, core], w_sems.at[n, 2 * y + core]
            )
            for y in range(NY)
            for core in range(2)
        ]

    def start(n, carry):
        for copy in columns(n):
            copy.start()
        return carry

    copies = []
    for i, (first, by) in enumerate(((0, 0), (0, NX - 1), (0, 1), (0, 2), (middle, 2))):
        along = pl.multiple_of((x[0] + by) % NX * cols, cols)
        rows = pieces[i].shape[0]
        copies.append(
            pltpu.make_async_copy(
                pieces[i], t_all.at[pl.ds(first, rows), pl.ds(along, cols)], t_sems.at[i]
            )
        )
    for copy in copies:
        copy.start()
    lax.fori_loop(0, tiles, start, 0)
    for copy in copies:
        copy.wait()

    def product(n):
        for copy in columns(n):
            copy.wait()
        tile = w_all[n].reshape(depth, wide)
        return jnp.dot(t_all[...], tile, preferred_element_type=jnp.float32)

    def main_tile(n, carry):
        total = product(n)
        value = total / (1.0 + jnp.exp(-total))
        main_out[:, pl.ds(pl.multiple_of(n * wide, wide), wide)] = value.astype(jnp.bfloat16)
        return carry

    lax.fori_loop(0, tiles - 1, main_tile, 0)
    extra_out[...] = product(tiles - 1)


def project(x, weights, pieces, rows, wide):
    cols = weights.shape[-1]
    depth = weights.size // cols
    main = cols - wide
    return pl.pallas_call(
        project_kernel,
        out_shape=(
            jax.ShapeDtypeStruct((rows, main), jnp.bfloat16),
            jax.ShapeDtypeStruct((rows, wide), jnp.float32),
        ),
        in_specs=[SCALARS, HBM] + [ANY] * 5,
        out_specs=(WHOLE,) * 2,
        scratch_shapes=[
            pltpu.VMEM((cols // wide, NY, NZ, 2, depth // (2 * NY * NZ), wide), jnp.bfloat16),
            pltpu.VMEM((rows, depth), jnp.bfloat16),
            pltpu.SemaphoreType.DMA((cols // wide, 2 * NY)),
            pltpu.SemaphoreType.DMA((5,)),
        ],
        compiler_params=pltpu.CompilerParams(vmem_limit_bytes=VMEM),
        cost_estimate=pl.CostEstimate(
            flops=2 * rows * depth * cols, bytes_accessed=2 * depth * (cols + rows), transcendentals=rows * main
        ),
        name="project",
    )(x, weights, *pieces)


def split_dot(left, right):
    high = left.astype(jnp.bfloat16)
    low = (left - high.astype(jnp.float32)).astype(jnp.bfloat16)
    return jnp.dot(high, right, preferred_element_type=jnp.float32) + jnp.dot(
        low, right, preferred_element_type=jnp.float32
    )


def local_kernel(inner, b_values, c_values, decay, decay_t, step_t, gain, live, out, factor):
    length = PAGE
    row = lax.broadcasted_iota(jnp.int32, (length, length), 0)
    column = lax.broadcasted_iota(jnp.int32, (length, length), 1)
    causal = row >= column
    first = lax.broadcasted_iota(jnp.int32, (length, 2 * HP), 1) < HP
    for member in range(decay.shape[0]):
        rows = slice(member * length, (member + 1) * length)
        crossing = lax.dot_general(
            c_values[rows, :],
            b_values[rows, :],
            (((1,), (1,)), ((), ())),
            preferred_element_type=jnp.float32,
        )
        fades = jnp.exp(decay[member])
        for pair in range(decay.shape[2] // 2):
            lanes = slice(pair * 2 * HP, (pair + 1) * 2 * HP)
            values = inner[rows, lanes]
            parts = []
            for head in (2 * pair, 2 * pair + 1):
                gaps = decay[member, :, head : head + 1] - decay_t[member, head : head + 1, :]
                gaps = jnp.where(causal, gaps, -jnp.inf)
                mixing = jnp.exp(gaps) * crossing * step_t[member, head : head + 1, :]
                parts.append(split_dot(mixing, values))
            local = jnp.where(first, parts[0], parts[1])
            local = local + gain[:, lanes] * values.astype(jnp.float32)
            out[rows, lanes] = local * live[rows, :]
            fade = jnp.where(first, fades[:, 2 * pair : 2 * pair + 1], fades[:, 2 * pair + 1 : 2 * pair + 2])
            factor[rows, lanes] = fade * live[rows, :]


def mix_locally(inner, b_values, c_values, decay, decay_t, step_t, gain, live):
    rows, cols = inner.shape
    return pl.pallas_call(
        local_kernel,
        out_shape=(jax.ShapeDtypeStruct((rows, cols), jnp.float32),) * 2,
        in_specs=[WHOLE] * 8,
        out_specs=(WHOLE,) * 2,
        compiler_params=pltpu.CompilerParams(vmem_limit_bytes=VMEM),
        cost_estimate=pl.CostEstimate(
            flops=8 * rows * PAGE * cols, bytes_accessed=6 * rows * cols, transcendentals=rows * PAGE * 32
        ),
        name="mix_locally",
    )(inner, b_values, c_values, decay, decay_t, step_t, gain, live)


def carry_kernel(
    sources, incoming, c_values, factor, local, out, held, factors, locals_, ready, in_sems, out_sems
):
    members = sources.shape[0]
    span = 2 * PAGE

    def rows_of(member):
        return pl.ds(member * PAGE, PAGE)

    def bring(member):
        rows = rows_of(member)
        return [
            pltpu.make_async_copy(factor.at[rows, :], factors.at[rows, :], in_sems.at[member, 1]),
            pltpu.make_async_copy(local.at[rows, :], locals_.at[rows, :], in_sems.at[member, 2]),
        ]

    def store(member):
        rows = rows_of(member)
        return pltpu.make_async_copy(ready.at[rows, :], out.at[rows, :], out_sems.at[member])

    for member in range(members):
        for page in range(SP):
            pltpu.make_async_copy(
                incoming.at[sources[member, page]], held.at[member * SP + page], in_sems.at[member, 0]
            ).start()
        for copy in bring(member):
            copy.start()
    for member in range(members):
        rows = rows_of(member)
        pages = pl.ds(member * SP, SP)
        pltpu.make_async_copy(incoming.at[pl.ds(0, SP)], held.at[pages], in_sems.at[member, 0]).wait()
        for copy in bring(member):
            copy.wait()
        for page in range(0, SP, 2):
            lanes = slice(page * 2 * HP, page * 2 * HP + span)
            pair = held[member * SP + page : member * SP + page + 2].reshape(span, NST)
            carried = lax.dot_general(
                c_values[rows, :], pair, (((1,), (1,)), ((), ())), preferred_element_type=jnp.float32
            )
            total = locals_[rows, lanes] + carried * factors[rows, lanes]
            ready[rows, lanes] = total.astype(jnp.bfloat16)
        store(member).start()
    for member in range(members):
        store(member).wait()


def carry_state(sources, incoming, c_values, factor, local):
    rows, cols = local.shape
    members = sources.shape[0]
    return pl.pallas_call(
        carry_kernel,
        out_shape=jax.ShapeDtypeStruct((rows, cols), jnp.bfloat16),
        in_specs=[SCALARS, HBM, WHOLE, HBM, HBM],
        out_specs=HBM,
        scratch_shapes=[
            pltpu.VMEM((members * SP,) + incoming.shape[1:], incoming.dtype),
            pltpu.VMEM((rows, cols), jnp.float32),
            pltpu.VMEM((rows, cols), jnp.float32),
            pltpu.VMEM((rows, cols), jnp.bfloat16),
            pltpu.SemaphoreType.DMA((members, 3)),
            pltpu.SemaphoreType.DMA((members,)),
        ],
        compiler_params=pltpu.CompilerParams(vmem_limit_bytes=VMEM),
        cost_estimate=pl.CostEstimate(
            flops=2 * rows * NST * cols, bytes_accessed=8 * rows * cols, transcendentals=0
        ),
        name="carry_state",
    )(sources, incoming, c_values, factor, local)


CHUNK = 8


def attend_kernel(sources, prefix, queries, fresh, live, incoming, out, stacked, held, top, total, sems):
    members, slots = sources.shape
    heads = queries.shape[1] // HD
    factor = math.log2(math.e) / math.sqrt(HD)
    nothing = -1e30

    def copy(member, slot):
        return pltpu.make_async_copy(
            incoming.at[sources[member, slot]],
            held.at[member, pl.ds(pl.multiple_of(slot * PAGE, PAGE), PAGE), :],
            sems.at[member, slot],
        )

    for member in range(members):

        def start(slot, carry):
            @pl.when(slot < prefix[member])
            def _():
                copy(member, slot).start()

            @pl.when(slot >= prefix[member])
            def _():
                held[member, pl.ds(pl.multiple_of(slot * PAGE, PAGE), PAGE), :] = jnp.zeros(
                    (PAGE, 2 * HD), held.dtype
                )

            return carry

        lax.fori_loop(0, slots, start, 0)

    wide = CHUNK * PAGE
    block = 2 * PAGE
    causal = lax.broadcasted_iota(jnp.int32, (block, PAGE), 0) % PAGE >= lax.broadcasted_iota(
        jnp.int32, (block, PAGE), 1
    )
    for member in range(members):
        rows = slice(member * PAGE, (member + 1) * PAGE)
        for head in range(heads):
            stacked[head * PAGE : (head + 1) * PAGE, :] = queries[rows, head * HD : (head + 1) * HD]
        new_keys = fresh[rows, :HD]
        new_values = jnp.concatenate([jnp.ones((PAGE, HD), jnp.bfloat16), fresh[rows, HD:]], axis=1)
        for part in range(heads // 2):
            at = slice(part * block, (part + 1) * block)
            scores = lax.dot_general(
                stacked[at, :], new_keys, (((1,), (1,)), ((), ())), preferred_element_type=jnp.float32
            )
            scores = jnp.where(causal, scores * factor, nothing)
            best = jnp.max(scores, axis=1, keepdims=True)
            weights = jnp.exp2(scores - best).astype(jnp.bfloat16)
            top[at, :] = jnp.broadcast_to(best, (block, HD))
            total[at, :] = jnp.dot(weights, new_values, preferred_element_type=jnp.float32)

        def chunk(index, carry):
            base = index * CHUNK

            def finish(slot, inside):
                @pl.when(base + slot < prefix[member])
                def _():
                    copy(member, base + slot).wait()

                return inside

            lax.fori_loop(0, CHUNK, finish, 0)
            span = pl.ds(pl.multiple_of(index * wide, wide), wide)
            keys = held[member, span, :HD]
            values = jnp.concatenate([jnp.ones((wide, HD), jnp.bfloat16), held[member, span, HD:]], axis=1)
            seen = index * wide + lax.broadcasted_iota(jnp.int32, (1, wide), 1) < prefix[member] * PAGE
            bias = jnp.where(seen, 0.0, nothing)
            for part in range(heads // 2):
                at = slice(part * block, (part + 1) * block)
                scores = lax.dot_general(
                    stacked[at, :], keys, (((1,), (1,)), ((), ())), preferred_element_type=jnp.float32
                )
                scores = scores * factor + bias
                before = top[at, :1]
                best = jnp.maximum(before, jnp.max(scores, axis=1, keepdims=True))
                weights = jnp.exp2(scores - best).astype(jnp.bfloat16)
                shrink = jnp.exp2(before - best)
                top[at, :] = jnp.broadcast_to(best, (block, HD))
                total[at, :] = total[at, :] * shrink + jnp.dot(
                    weights, values, preferred_element_type=jnp.float32
                )
            return carry

        lax.fori_loop(0, (prefix[member] + CHUNK - 1) // CHUNK, chunk, 0)
        for head in range(heads):
            at = slice(head * PAGE, (head + 1) * PAGE)
            mixed = total[at, HD:] / total[at, :HD] * live[rows, :]
            out[rows, head * HD : (head + 1) * HD] = mixed.astype(jnp.bfloat16)


def attend(sources, prefix, queries, fresh, live, incoming):
    rows, cols = queries.shape
    members, slots = sources.shape
    heads = cols // HD
    return pl.pallas_call(
        attend_kernel,
        out_shape=jax.ShapeDtypeStruct((rows, cols), jnp.bfloat16),
        in_specs=[SCALARS, SCALARS] + [WHOLE] * 3 + [HBM],
        out_specs=WHOLE,
        scratch_shapes=[
            pltpu.VMEM((heads * PAGE, HD), jnp.bfloat16),
            pltpu.VMEM((members, slots * PAGE, 2 * HD), jnp.bfloat16),
            pltpu.VMEM((heads * PAGE, HD), jnp.float32),
            pltpu.VMEM((heads * PAGE, 2 * HD), jnp.float32),
            pltpu.SemaphoreType.DMA((members, slots)),
        ],
        compiler_params=pltpu.CompilerParams(vmem_limit_bytes=VMEM),
        cost_estimate=pl.CostEstimate(
            flops=4 * rows * cols * slots * PAGE,
            bytes_accessed=members * slots * PAGE * 4 * HD,
            transcendentals=rows * heads * slots * PAGE,
        ),
        name="attend",
    )(sources, prefix, queries, fresh, live, incoming)


def gather_tokens(tokens):
    middle = tokens.shape[0] // 2
    up, down = around_x(tokens, 1), around_x(tokens, -1)
    return [tokens, up, down, around_x(up[:middle], 1), around_x(down[middle:], -1)]


def body(
    tokens,
    x_weight,
    bc_weight,
    step_weight,
    step_bias,
    decay_log,
    skip_gain,
    queries,
    new_keyvals,
    page_pool,
    page_table,
    prefix_pages,
    new_counts,
):
    owners = lax.axis_size(DP)
    x = lax.axis_index("tensor")
    seq_dev = page_table.shape[0]
    pool_size = page_pool.shape[0]
    rows = tokens.shape[0]
    length = rows // seq_dev
    heads = step_bias.shape[0]

    sources = page_table // pool_size
    places = page_table % pool_size
    names = jnp.arange(owners, dtype=jnp.int32)[:, None]

    def wanted(part):
        asked = sources[:, part].reshape(1, -1) == names
        return jnp.max(jnp.where(asked, places[:, part].reshape(1, -1), 0), axis=1)

    asks = jnp.stack([wanted(slice(SP, None)), wanted(slice(0, SP))], axis=1)
    asks = jnp.pad(asks, ((0, 0), (0, 126))).reshape(owners, 1, 128)
    extra = bc_weight.shape[1]
    x_weight, bc_weight, step_weight, asks = lax.optimization_barrier(
        (x_weight, bc_weight, step_weight, asks)
    )
    step_wide = jnp.pad(step_weight, ((0, 0), (0, extra - heads)))
    weights = jnp.concatenate([x_weight, bc_weight, step_wide], axis=1)
    weights = lax.all_gather(weights, "z", axis=0)
    picks = lax.all_to_all(asks, DP, split_axis=0, concat_axis=0, tiled=True)
    kv_out = pack_pages(picks, 0, page_pool)
    kv_in = lax.all_to_all(kv_out, DP, split_axis=0, concat_axis=0, tiled=True)
    later_pool, _ = lax.optimization_barrier((page_pool, kv_out))
    state_out = pack_pages(picks, 1, later_pool)
    state_in = lax.all_to_all(state_out, DP, split_axis=0, concat_axis=0, tiled=True)

    weights, _ = lax.optimization_barrier((weights, state_out))
    weights = lax.all_gather(weights, ("y", "core"), axis=0)
    weights = weights.reshape((NY, 2) + weights.shape[1:])
    tokens, _ = lax.optimization_barrier((tokens, kv_out))
    inner, extras = project(
        x.reshape(1).astype(jnp.int32), weights, gather_tokens(tokens), rows, 2 * extra
    )
    columns = extras[:, :extra].astype(jnp.bfloat16)
    step_raw = extras[:, extra : extra + heads]
    around = jnp.stack([columns] + [around_x(columns, -k) for k in range(1, NX)])
    quarters = [lax.dynamic_index_in_dim(around, (t - x) % NX, 0, keepdims=False) for t in range(NX)]
    b_values = jnp.concatenate(quarters[:2], axis=1)
    c_values = jnp.concatenate(quarters[2:], axis=1)

    live = (jnp.arange(length)[None, :] < new_counts[:, None]).astype(jnp.float32)
    step = jax.nn.softplus(step_raw + step_bias[None, :]).reshape(seq_dev, length, heads)
    step = step * live[:, :, None]
    decay = jnp.cumsum(-step * jnp.exp(decay_log)[None, None, :], axis=1)
    gain = jnp.repeat(skip_gain, HP)[None, :]
    live_column = live.reshape(rows, 1)
    local, factor = mix_locally(
        inner, b_values, c_values, decay, decay.transpose(0, 2, 1), step.transpose(0, 2, 1), gain, live_column
    )
    attention_out = attend(
        sources[:, SP:], prefix_pages, queries, new_keyvals, live_column, kv_in
    )
    mamba_out = carry_state(sources[:, :SP], state_in, c_values, factor, local)
    return (mamba_out, attention_out)


def solution(mesh):
    split = Mesh(mesh.devices.reshape(NY, NZ, 2, NX), DP + ("tensor",))
    placed = (
        P(DP, "tensor"),
        P(DP, "tensor"),
        P(DP, "tensor"),
        P(DP, "tensor"),
        P("tensor"),
        P("tensor"),
        P("tensor"),
        P(DP, "tensor"),
        P(DP, "tensor"),
        P(DP, None, "tensor"),
        P(DP, None),
        P(DP),
        P(DP),
    )
    return jax.shard_map(
        body,
        mesh=split,
        in_specs=placed,
        out_specs=(P(DP, "tensor"), P(DP, "tensor")),
        check_vma=False,
    )
```

```python
import functools
import math

import jax
import jax.numpy as jnp
from jax import lax
from jax.experimental import pallas as pl
from jax.experimental.pallas import tpu as pltpu
from jax.sharding import Mesh
from jax.sharding import PartitionSpec as P

HP = 64
NST = 256
HD = 128
PAGE = 128
SP = 16
NY = 4
NZ = 8
NX = 4
DP = ("y", "z", "core")
VMEM = 62 * 1024 * 1024
ANY = pl.BlockSpec(memory_space=pl.ANY)
HBM = pl.BlockSpec(memory_space=pltpu.HBM)
WHOLE = pl.BlockSpec(memory_space=pltpu.VMEM)
SCALARS = pl.BlockSpec(memory_space=pltpu.SMEM)


def around_x(array, by):
    return lax.ppermute(array, "tensor", [(i, (i + by) % NX) for i in range(NX)])


def pack_kernel(column, picks, pool, out, held, in_sems, out_sems):
    owners = out.shape[0]
    parts = in_sems.shape[0]
    span = owners // parts

    def fetch(r, part):
        pltpu.make_async_copy(pool.at[picks[r, 0, column]], held.at[r], in_sems.at[part]).start()
        return part

    def store(part):
        rows = pl.ds(part * span, span)
        return pltpu.make_async_copy(held.at[rows], out.at[rows], out_sems.at[part])

    for part in range(parts):
        lax.fori_loop(part * span, (part + 1) * span, fetch, part, unroll=8)
    for part in range(parts):
        rows = pl.ds(part * span, span)
        pltpu.make_async_copy(pool.at[pl.ds(0, span)], held.at[rows], in_sems.at[part]).wait()
        store(part).start()
    for part in range(parts):
        store(part).wait()


def pack_pages(picks, column, pool, weight=1):
    owners = picks.shape[0]
    page = pool.shape[1:]
    return pl.pallas_call(
        functools.partial(pack_kernel, column),
        out_shape=jax.ShapeDtypeStruct((owners,) + page, pool.dtype),
        in_specs=[SCALARS, HBM],
        out_specs=HBM,
        scratch_shapes=[
            pltpu.VMEM((owners,) + page, pool.dtype),
            pltpu.SemaphoreType.DMA((4,)),
            pltpu.SemaphoreType.DMA((4,)),
        ],
        compiler_params=pltpu.CompilerParams(vmem_limit_bytes=VMEM),
        cost_estimate=pl.CostEstimate(
            flops=0, bytes_accessed=4 * weight * owners * page[0] * page[1], transcendentals=0
        ),
        name="pack_pages",
    )(picks, pool)


def project_kernel(x, weights, *refs):
    pieces = refs[:5]
    main_out, extra_out, w_all, t_all, w_sems, t_sems = refs[5:]
    tiles, wide = w_all.shape[0], w_all.shape[5]
    depth = t_all.shape[1]
    cols = pieces[0].shape[1]
    middle = pieces[3].shape[0]

    def columns(n):
        along = pl.ds(pl.multiple_of(n * wide, wide), wide)
        return [
            pltpu.make_async_copy(
                weights.at[y, core, :, :, along], w_all.at[n, y, :, core], w_sems.at[n, 2 * y + core]
            )
            for y in range(NY)
            for core in range(2)
        ]

    def start(n, carry):
        for copy in columns(n):
            copy.start()
        return carry

    copies = []
    for i, (first, by) in enumerate(((0, 0), (0, NX - 1), (0, 1), (0, 2), (middle, 2))):
        along = pl.multiple_of((x[0] + by) % NX * cols, cols)
        rows = pieces[i].shape[0]
        copies.append(
            pltpu.make_async_copy(
                pieces[i], t_all.at[pl.ds(first, rows), pl.ds(along, cols)], t_sems.at[i]
            )
        )
    for copy in copies:
        copy.start()
    lax.fori_loop(0, tiles, start, 0)
    for copy in copies:
        copy.wait()

    def product(n):
        for copy in columns(n):
            copy.wait()
        tile = w_all[n].reshape(depth, wide)
        return jnp.dot(t_all[...], tile, preferred_element_type=jnp.float32)

    def main_tile(n, carry):
        total = product(n)
        value = total / (1.0 + jnp.exp(-total))
        main_out[:, pl.ds(pl.multiple_of(n * wide, wide), wide)] = value.astype(jnp.bfloat16)
        return carry

    lax.fori_loop(0, tiles - 1, main_tile, 0)
    extra_out[...] = product(tiles - 1)


def project(x, weights, pieces, rows, wide):
    cols = weights.shape[-1]
    depth = weights.size // cols
    main = cols - wide
    return pl.pallas_call(
        project_kernel,
        out_shape=(
            jax.ShapeDtypeStruct((rows, main), jnp.bfloat16),
            jax.ShapeDtypeStruct((rows, wide), jnp.float32),
        ),
        in_specs=[SCALARS, HBM] + [ANY] * 5,
        out_specs=(WHOLE,) * 2,
        scratch_shapes=[
            pltpu.VMEM((cols // wide, NY, NZ, 2, depth // (2 * NY * NZ), wide), jnp.bfloat16),
            pltpu.VMEM((rows, depth), jnp.bfloat16),
            pltpu.SemaphoreType.DMA((cols // wide, 2 * NY)),
            pltpu.SemaphoreType.DMA((5,)),
        ],
        compiler_params=pltpu.CompilerParams(vmem_limit_bytes=VMEM),
        cost_estimate=pl.CostEstimate(
            flops=2 * rows * depth * cols, bytes_accessed=2 * depth * (cols + rows), transcendentals=rows * main
        ),
        name="project",
    )(x, weights, *pieces)


def split_dot(left, right):
    high = left.astype(jnp.bfloat16)
    low = (left - high.astype(jnp.float32)).astype(jnp.bfloat16)
    return jnp.dot(high, right, preferred_element_type=jnp.float32) + jnp.dot(
        low, right, preferred_element_type=jnp.float32
    )


def local_kernel(inner, b_values, c_values, decay, decay_t, step_t, gain, live, out, factor):
    length = PAGE
    row = lax.broadcasted_iota(jnp.int32, (length, length), 0)
    column = lax.broadcasted_iota(jnp.int32, (length, length), 1)
    causal = row >= column
    first = lax.broadcasted_iota(jnp.int32, (length, 2 * HP), 1) < HP
    for member in range(decay.shape[0]):
        rows = slice(member * length, (member + 1) * length)
        crossing = lax.dot_general(
            c_values[rows, :],
            b_values[rows, :],
            (((1,), (1,)), ((), ())),
            preferred_element_type=jnp.float32,
        )
        fades = jnp.exp(decay[member])
        for pair in range(decay.shape[2] // 2):
            lanes = slice(pair * 2 * HP, (pair + 1) * 2 * HP)
            values = inner[rows, lanes]
            parts = []
            for head in (2 * pair, 2 * pair + 1):
                gaps = decay[member, :, head : head + 1] - decay_t[member, head : head + 1, :]
                gaps = jnp.where(causal, gaps, -jnp.inf)
                mixing = jnp.exp(gaps) * crossing * step_t[member, head : head + 1, :]
                parts.append(split_dot(mixing, values))
            local = jnp.where(first, parts[0], parts[1])
            local = local + gain[:, lanes] * values.astype(jnp.float32)
            out[rows, lanes] = local * live[rows, :]
            fade = jnp.where(first, fades[:, 2 * pair : 2 * pair + 1], fades[:, 2 * pair + 1 : 2 * pair + 2])
            factor[rows, lanes] = fade * live[rows, :]


def mix_locally(inner, b_values, c_values, decay, decay_t, step_t, gain, live):
    rows, cols = inner.shape
    return pl.pallas_call(
        local_kernel,
        out_shape=(jax.ShapeDtypeStruct((rows, cols), jnp.float32),) * 2,
        in_specs=[WHOLE] * 8,
        out_specs=(WHOLE,) * 2,
        compiler_params=pltpu.CompilerParams(vmem_limit_bytes=VMEM),
        cost_estimate=pl.CostEstimate(
            flops=8 * rows * PAGE * cols, bytes_accessed=6 * rows * cols, transcendentals=rows * PAGE * 32
        ),
        name="mix_locally",
    )(inner, b_values, c_values, decay, decay_t, step_t, gain, live)


def carry_kernel(
    sources, incoming, c_values, factor, local, out, held, factors, locals_, ready, in_sems, out_sems
):
    members = sources.shape[0]
    span = 2 * PAGE

    def rows_of(member):
        return pl.ds(member * PAGE, PAGE)

    def bring(member):
        rows = rows_of(member)
        return [
            pltpu.make_async_copy(factor.at[rows, :], factors.at[rows, :], in_sems.at[member, 1]),
            pltpu.make_async_copy(local.at[rows, :], locals_.at[rows, :], in_sems.at[member, 2]),
        ]

    def store(member):
        rows = rows_of(member)
        return pltpu.make_async_copy(ready.at[rows, :], out.at[rows, :], out_sems.at[member])

    for member in range(members):
        for page in range(SP):
            pltpu.make_async_copy(
                incoming.at[sources[member, page]], held.at[member * SP + page], in_sems.at[member, 0]
            ).start()
        for copy in bring(member):
            copy.start()
    for member in range(members):
        rows = rows_of(member)
        pages = pl.ds(member * SP, SP)
        pltpu.make_async_copy(incoming.at[pl.ds(0, SP)], held.at[pages], in_sems.at[member, 0]).wait()
        for copy in bring(member):
            copy.wait()
        for page in range(0, SP, 2):
            lanes = slice(page * 2 * HP, page * 2 * HP + span)
            pair = held[member * SP + page : member * SP + page + 2].reshape(span, NST)
            carried = lax.dot_general(
                c_values[rows, :], pair, (((1,), (1,)), ((), ())), preferred_element_type=jnp.float32
            )
            total = locals_[rows, lanes] + carried * factors[rows, lanes]
            ready[rows, lanes] = total.astype(jnp.bfloat16)
        store(member).start()
    for member in range(members):
        store(member).wait()


def carry_state(sources, incoming, c_values, factor, local):
    rows, cols = local.shape
    members = sources.shape[0]
    return pl.pallas_call(
        carry_kernel,
        out_shape=jax.ShapeDtypeStruct((rows, cols), jnp.bfloat16),
        in_specs=[SCALARS, HBM, WHOLE, HBM, HBM],
        out_specs=HBM,
        scratch_shapes=[
            pltpu.VMEM((members * SP,) + incoming.shape[1:], incoming.dtype),
            pltpu.VMEM((rows, cols), jnp.float32),
            pltpu.VMEM((rows, cols), jnp.float32),
            pltpu.VMEM((rows, cols), jnp.bfloat16),
            pltpu.SemaphoreType.DMA((members, 3)),
            pltpu.SemaphoreType.DMA((members,)),
        ],
        compiler_params=pltpu.CompilerParams(vmem_limit_bytes=VMEM),
        cost_estimate=pl.CostEstimate(
            flops=2 * rows * NST * cols, bytes_accessed=8 * rows * cols, transcendentals=0
        ),
        name="carry_state",
    )(sources, incoming, c_values, factor, local)


CHUNK = 8


def attend_kernel(sources, prefix, queries, fresh, live, incoming, out, stacked, held, top, total, sems):
    members, slots = sources.shape
    heads = queries.shape[1] // HD
    factor = math.log2(math.e) / math.sqrt(HD)
    nothing = -1e30

    def copy(member, slot):
        return pltpu.make_async_copy(
            incoming.at[sources[member, slot]],
            held.at[member, pl.ds(pl.multiple_of(slot * PAGE, PAGE), PAGE), :],
            sems.at[member, slot],
        )

    for member in range(members):

        def start(slot, carry):
            @pl.when(slot < prefix[member])
            def _():
                copy(member, slot).start()

            @pl.when(slot >= prefix[member])
            def _():
                held[member, pl.ds(pl.multiple_of(slot * PAGE, PAGE), PAGE), :] = jnp.zeros(
                    (PAGE, 2 * HD), held.dtype
                )

            return carry

        lax.fori_loop(0, slots, start, 0)

    wide = CHUNK * PAGE
    block = 2 * PAGE
    causal = lax.broadcasted_iota(jnp.int32, (block, PAGE), 0) % PAGE >= lax.broadcasted_iota(
        jnp.int32, (block, PAGE), 1
    )
    for member in range(members):
        rows = slice(member * PAGE, (member + 1) * PAGE)
        for head in range(heads):
            stacked[head * PAGE : (head + 1) * PAGE, :] = queries[rows, head * HD : (head + 1) * HD]
        new_keys = fresh[rows, :HD]
        new_values = jnp.concatenate([jnp.ones((PAGE, HD), jnp.bfloat16), fresh[rows, HD:]], axis=1)
        for part in range(heads // 2):
            at = slice(part * block, (part + 1) * block)
            scores = lax.dot_general(
                stacked[at, :], new_keys, (((1,), (1,)), ((), ())), preferred_element_type=jnp.float32
            )
            scores = jnp.where(causal, scores * factor, nothing)
            best = jnp.max(scores, axis=1, keepdims=True)
            weights = jnp.exp2(scores - best).astype(jnp.bfloat16)
            top[at, :] = jnp.broadcast_to(best, (block, HD))
            total[at, :] = jnp.dot(weights, new_values, preferred_element_type=jnp.float32)

        def chunk(index, carry):
            base = index * CHUNK

            def finish(slot, inside):
                @pl.when(base + slot < prefix[member])
                def _():
                    copy(member, base + slot).wait()

                return inside

            lax.fori_loop(0, CHUNK, finish, 0)
            span = pl.ds(pl.multiple_of(index * wide, wide), wide)
            keys = held[member, span, :HD]
            values = jnp.concatenate([jnp.ones((wide, HD), jnp.bfloat16), held[member, span, HD:]], axis=1)
            seen = index * wide + lax.broadcasted_iota(jnp.int32, (1, wide), 1) < prefix[member] * PAGE
            bias = jnp.where(seen, 0.0, nothing)
            for part in range(heads // 2):
                at = slice(part * block, (part + 1) * block)
                scores = lax.dot_general(
                    stacked[at, :], keys, (((1,), (1,)), ((), ())), preferred_element_type=jnp.float32
                )
                scores = scores * factor + bias
                before = top[at, :1]
                best = jnp.maximum(before, jnp.max(scores, axis=1, keepdims=True))
                weights = jnp.exp2(scores - best).astype(jnp.bfloat16)
                shrink = jnp.exp2(before - best)
                top[at, :] = jnp.broadcast_to(best, (block, HD))
                total[at, :] = total[at, :] * shrink + jnp.dot(
                    weights, values, preferred_element_type=jnp.float32
                )
            return carry

        lax.fori_loop(0, (prefix[member] + CHUNK - 1) // CHUNK, chunk, 0)
        for head in range(heads):
            at = slice(head * PAGE, (head + 1) * PAGE)
            mixed = total[at, HD:] / total[at, :HD] * live[rows, :]
            out[rows, head * HD : (head + 1) * HD] = mixed.astype(jnp.bfloat16)


def attend(sources, prefix, queries, fresh, live, incoming):
    rows, cols = queries.shape
    members, slots = sources.shape
    heads = cols // HD
    return pl.pallas_call(
        attend_kernel,
        out_shape=jax.ShapeDtypeStruct((rows, cols), jnp.bfloat16),
        in_specs=[SCALARS, SCALARS] + [WHOLE] * 3 + [HBM],
        out_specs=WHOLE,
        scratch_shapes=[
            pltpu.VMEM((heads * PAGE, HD), jnp.bfloat16),
            pltpu.VMEM((members, slots * PAGE, 2 * HD), jnp.bfloat16),
            pltpu.VMEM((heads * PAGE, HD), jnp.float32),
            pltpu.VMEM((heads * PAGE, 2 * HD), jnp.float32),
            pltpu.SemaphoreType.DMA((members, slots)),
        ],
        compiler_params=pltpu.CompilerParams(vmem_limit_bytes=VMEM),
        cost_estimate=pl.CostEstimate(
            flops=400 * rows * cols * slots * PAGE,
            bytes_accessed=members * slots * PAGE * 4 * HD,
            transcendentals=rows * heads * slots * PAGE,
        ),
        name="attend",
    )(sources, prefix, queries, fresh, live, incoming)


def gather_tokens(tokens):
    middle = tokens.shape[0] // 2
    up, down = around_x(tokens, 1), around_x(tokens, -1)
    return [tokens, up, down, around_x(up[:middle], 1), around_x(down[middle:], -1)]


def body(
    tokens,
    x_weight,
    bc_weight,
    step_weight,
    step_bias,
    decay_log,
    skip_gain,
    queries,
    new_keyvals,
    page_pool,
    page_table,
    prefix_pages,
    new_counts,
):
    owners = lax.axis_size(DP)
    x = lax.axis_index("tensor")
    seq_dev = page_table.shape[0]
    pool_size = page_pool.shape[0]
    rows = tokens.shape[0]
    length = rows // seq_dev
    heads = step_bias.shape[0]

    sources = page_table // pool_size
    places = page_table % pool_size
    names = jnp.arange(owners, dtype=jnp.int32)[:, None]

    def wanted(part):
        asked = sources[:, part].reshape(1, -1) == names
        return jnp.max(jnp.where(asked, places[:, part].reshape(1, -1), 0), axis=1)

    asks = jnp.stack([wanted(slice(SP, None)), wanted(slice(0, SP))], axis=1)
    asks = jnp.pad(asks, ((0, 0), (0, 126))).reshape(owners, 1, 128)
    extra = bc_weight.shape[1]
    x_weight, bc_weight, step_weight, asks = lax.optimization_barrier(
        (x_weight, bc_weight, step_weight, asks)
    )
    step_wide = jnp.pad(step_weight, ((0, 0), (0, extra - heads)))
    weights = jnp.concatenate([x_weight, bc_weight, step_wide], axis=1)
    weights = lax.all_gather(weights, "z", axis=0)
    picks = lax.all_to_all(asks, DP, split_axis=0, concat_axis=0, tiled=True)
    kv_out = pack_pages(picks, 0, page_pool, 0)
    kv_in = lax.all_to_all(kv_out, DP, split_axis=0, concat_axis=0, tiled=True)
    later_pool, _, weights = lax.optimization_barrier((page_pool, kv_out, weights))
    state_out = pack_pages(picks, 1, later_pool, 100)
    state_in = lax.all_to_all(state_out, DP, split_axis=0, concat_axis=0, tiled=True)

    weights, _ = lax.optimization_barrier((weights, state_out))
    weights = lax.all_gather(weights, ("y", "core"), axis=0)
    weights = weights.reshape((NY, 2) + weights.shape[1:])
    tokens, _ = lax.optimization_barrier((tokens, kv_in))
    inner, extras = project(
        x.reshape(1).astype(jnp.int32), weights, gather_tokens(tokens), rows, 2 * extra
    )
    columns = extras[:, :extra].astype(jnp.bfloat16)
    step_raw = extras[:, extra : extra + heads]
    around = jnp.stack([columns] + [around_x(columns, -k) for k in range(1, NX)])
    quarters = [lax.dynamic_index_in_dim(around, (t - x) % NX, 0, keepdims=False) for t in range(NX)]
    b_values = jnp.concatenate(quarters[:2], axis=1)
    c_values = jnp.concatenate(quarters[2:], axis=1)

    live = (jnp.arange(length)[None, :] < new_counts[:, None]).astype(jnp.float32)
    step = jax.nn.softplus(step_raw + step_bias[None, :]).reshape(seq_dev, length, heads)
    step = step * live[:, :, None]
    decay = jnp.cumsum(-step * jnp.exp(decay_log)[None, None, :], axis=1)
    gain = jnp.repeat(skip_gain, HP)[None, :]
    live_column = live.reshape(rows, 1)
    local, factor = mix_locally(
        inner, b_values, c_values, decay, decay.transpose(0, 2, 1), step.transpose(0, 2, 1), gain, live_column
    )
    attention_out = attend(
        sources[:, SP:], prefix_pages, queries, new_keyvals, live_column, kv_in
    )
    mamba_out = carry_state(sources[:, :SP], state_in, c_values, factor, local)
    return (mamba_out, attention_out)


def solution(mesh):
    split = Mesh(mesh.devices.reshape(NY, NZ, 2, NX), DP + ("tensor",))
    placed = (
        P(DP, "tensor"),
        P(DP, "tensor"),
        P(DP, "tensor"),
        P(DP, "tensor"),
        P("tensor"),
        P("tensor"),
        P("tensor"),
        P(DP, "tensor"),
        P(DP, "tensor"),
        P(DP, None, "tensor"),
        P(DP, None),
        P(DP),
        P(DP),
    )
    return jax.shard_map(
        body,
        mesh=split,
        in_specs=placed,
        out_specs=(P(DP, "tensor"), P(DP, "tensor")),
        check_vma=False,
    )
```

```python
import functools
import math

import jax
import jax.numpy as jnp
from jax import lax
from jax.experimental import pallas as pl
from jax.experimental.pallas import tpu as pltpu
from jax.sharding import Mesh
from jax.sharding import PartitionSpec as P

HP = 64
NST = 256
HD = 128
PAGE = 128
SP = 16
NY = 4
NZ = 8
NX = 4
DP = ("y", "z", "core")
VMEM = 62 * 1024 * 1024
ANY = pl.BlockSpec(memory_space=pl.ANY)
HBM = pl.BlockSpec(memory_space=pltpu.HBM)
WHOLE = pl.BlockSpec(memory_space=pltpu.VMEM)
SCALARS = pl.BlockSpec(memory_space=pltpu.SMEM)


def around_x(array, by):
    return lax.ppermute(array, "tensor", [(i, (i + by) % NX) for i in range(NX)])


def pack_kernel(column, picks, pool, out, held, in_sems, out_sems):
    owners = out.shape[0]
    parts = in_sems.shape[0]
    span = owners // parts

    def fetch(r, part):
        pltpu.make_async_copy(pool.at[picks[r, 0, column]], held.at[r], in_sems.at[part]).start()
        return part

    def store(part):
        rows = pl.ds(part * span, span)
        return pltpu.make_async_copy(held.at[rows], out.at[rows], out_sems.at[part])

    for part in range(parts):
        lax.fori_loop(part * span, (part + 1) * span, fetch, part, unroll=8)
    for part in range(parts):
        rows = pl.ds(part * span, span)
        pltpu.make_async_copy(pool.at[pl.ds(0, span)], held.at[rows], in_sems.at[part]).wait()
        store(part).start()
    for part in range(parts):
        store(part).wait()


def pack_pages(picks, column, pool, weight=1):
    owners = picks.shape[0]
    page = pool.shape[1:]
    return pl.pallas_call(
        functools.partial(pack_kernel, column),
        out_shape=jax.ShapeDtypeStruct((owners,) + page, pool.dtype),
        in_specs=[SCALARS, HBM],
        out_specs=HBM,
        scratch_shapes=[
            pltpu.VMEM((owners,) + page, pool.dtype),
            pltpu.SemaphoreType.DMA((4,)),
            pltpu.SemaphoreType.DMA((4,)),
        ],
        compiler_params=pltpu.CompilerParams(vmem_limit_bytes=VMEM),
        cost_estimate=pl.CostEstimate(
            flops=0, bytes_accessed=4 * weight * owners * page[0] * page[1], transcendentals=0
        ),
        name="pack_pages",
    )(picks, pool)


def project_kernel(x, weights, *refs):
    pieces = refs[:5]
    main_out, extra_out, w_all, t_all, w_sems, t_sems = refs[5:]
    tiles, wide = w_all.shape[0], w_all.shape[5]
    depth = t_all.shape[1]
    cols = pieces[0].shape[1]
    middle = pieces[3].shape[0]

    def columns(n):
        along = pl.ds(pl.multiple_of(n * wide, wide), wide)
        return [
            pltpu.make_async_copy(
                weights.at[y, core, :, :, along], w_all.at[n, y, :, core], w_sems.at[n, 2 * y + core]
            )
            for y in range(NY)
            for core in range(2)
        ]

    def start(n, carry):
        for copy in columns(n):
            copy.start()
        return carry

    copies = []
    for i, (first, by) in enumerate(((0, 0), (0, NX - 1), (0, 1), (0, 2), (middle, 2))):
        along = pl.multiple_of((x[0] + by) % NX * cols, cols)
        rows = pieces[i].shape[0]
        copies.append(
            pltpu.make_async_copy(
                pieces[i], t_all.at[pl.ds(first, rows), pl.ds(along, cols)], t_sems.at[i]
            )
        )
    for copy in copies:
        copy.start()
    lax.fori_loop(0, tiles, start, 0)
    for copy in copies:
        copy.wait()

    def product(n):
        for copy in columns(n):
            copy.wait()
        tile = w_all[n].reshape(depth, wide)
        return jnp.dot(t_all[...], tile, preferred_element_type=jnp.float32)

    def main_tile(n, carry):
        total = product(n)
        value = total / (1.0 + jnp.exp(-total))
        main_out[:, pl.ds(pl.multiple_of(n * wide, wide), wide)] = value.astype(jnp.bfloat16)
        return carry

    lax.fori_loop(0, tiles - 1, main_tile, 0)
    extra_out[...] = product(tiles - 1)


def project(x, weights, pieces, rows, wide):
    cols = weights.shape[-1]
    depth = weights.size // cols
    main = cols - wide
    return pl.pallas_call(
        project_kernel,
        out_shape=(
            jax.ShapeDtypeStruct((rows, main), jnp.bfloat16),
            jax.ShapeDtypeStruct((rows, wide), jnp.float32),
        ),
        in_specs=[SCALARS, HBM] + [ANY] * 5,
        out_specs=(WHOLE,) * 2,
        scratch_shapes=[
            pltpu.VMEM((cols // wide, NY, NZ, 2, depth // (2 * NY * NZ), wide), jnp.bfloat16),
            pltpu.VMEM((rows, depth), jnp.bfloat16),
            pltpu.SemaphoreType.DMA((cols // wide, 2 * NY)),
            pltpu.SemaphoreType.DMA((5,)),
        ],
        compiler_params=pltpu.CompilerParams(vmem_limit_bytes=VMEM),
        cost_estimate=pl.CostEstimate(
            flops=2 * rows * depth * cols, bytes_accessed=2 * depth * (cols + rows), transcendentals=rows * main
        ),
        name="project",
    )(x, weights, *pieces)


def split_dot(left, right):
    high = left.astype(jnp.bfloat16)
    low = (left - high.astype(jnp.float32)).astype(jnp.bfloat16)
    return jnp.dot(high, right, preferred_element_type=jnp.float32) + jnp.dot(
        low, right, preferred_element_type=jnp.float32
    )


def local_kernel(inner, b_values, c_values, decay, decay_t, step_t, gain, live, out, factor):
    length = PAGE
    row = lax.broadcasted_iota(jnp.int32, (length, length), 0)
    column = lax.broadcasted_iota(jnp.int32, (length, length), 1)
    causal = row >= column
    first = lax.broadcasted_iota(jnp.int32, (length, 2 * HP), 1) < HP
    for member in range(decay.shape[0]):
        rows = slice(member * length, (member + 1) * length)
        crossing = lax.dot_general(
            c_values[rows, :],
            b_values[rows, :],
            (((1,), (1,)), ((), ())),
            preferred_element_type=jnp.float32,
        )
        fades = jnp.exp(decay[member])
        for pair in range(decay.shape[2] // 2):
            lanes = slice(pair * 2 * HP, (pair + 1) * 2 * HP)
            values = inner[rows, lanes]
            parts = []
            for head in (2 * pair, 2 * pair + 1):
                gaps = decay[member, :, head : head + 1] - decay_t[member, head : head + 1, :]
                gaps = jnp.where(causal, gaps, -jnp.inf)
                mixing = jnp.exp(gaps) * crossing * step_t[member, head : head + 1, :]
                parts.append(split_dot(mixing, values))
            local = jnp.where(first, parts[0], parts[1])
            local = local + gain[:, lanes] * values.astype(jnp.float32)
            out[rows, lanes] = local * live[rows, :]
            fade = jnp.where(first, fades[:, 2 * pair : 2 * pair + 1], fades[:, 2 * pair + 1 : 2 * pair + 2])
            factor[rows, lanes] = fade * live[rows, :]


def mix_locally(inner, b_values, c_values, decay, decay_t, step_t, gain, live):
    rows, cols = inner.shape
    return pl.pallas_call(
        local_kernel,
        out_shape=(jax.ShapeDtypeStruct((rows, cols), jnp.float32),) * 2,
        in_specs=[WHOLE] * 8,
        out_specs=(WHOLE,) * 2,
        compiler_params=pltpu.CompilerParams(vmem_limit_bytes=VMEM),
        cost_estimate=pl.CostEstimate(
            flops=8 * rows * PAGE * cols, bytes_accessed=6 * rows * cols, transcendentals=rows * PAGE * 32
        ),
        name="mix_locally",
    )(inner, b_values, c_values, decay, decay_t, step_t, gain, live)


def carry_kernel(
    sources, incoming, c_values, factor, local, out, held, factors, locals_, ready, in_sems, out_sems
):
    members = sources.shape[0]
    span = 2 * PAGE

    def rows_of(member):
        return pl.ds(member * PAGE, PAGE)

    def bring(member):
        rows = rows_of(member)
        return [
            pltpu.make_async_copy(factor.at[rows, :], factors.at[rows, :], in_sems.at[member, 1]),
            pltpu.make_async_copy(local.at[rows, :], locals_.at[rows, :], in_sems.at[member, 2]),
        ]

    def store(member):
        rows = rows_of(member)
        return pltpu.make_async_copy(ready.at[rows, :], out.at[rows, :], out_sems.at[member])

    for member in range(members):
        for page in range(SP):
            pltpu.make_async_copy(
                incoming.at[sources[member, page]], held.at[member * SP + page], in_sems.at[member, 0]
            ).start()
        for copy in bring(member):
            copy.start()
    for member in range(members):
        rows = rows_of(member)
        pages = pl.ds(member * SP, SP)
        pltpu.make_async_copy(incoming.at[pl.ds(0, SP)], held.at[pages], in_sems.at[member, 0]).wait()
        for copy in bring(member):
            copy.wait()
        for page in range(0, SP, 2):
            lanes = slice(page * 2 * HP, page * 2 * HP + span)
            pair = held[member * SP + page : member * SP + page + 2].reshape(span, NST)
            carried = lax.dot_general(
                c_values[rows, :], pair, (((1,), (1,)), ((), ())), preferred_element_type=jnp.float32
            )
            total = locals_[rows, lanes] + carried * factors[rows, lanes]
            ready[rows, lanes] = total.astype(jnp.bfloat16)
        store(member).start()
    for member in range(members):
        store(member).wait()


def carry_state(sources, incoming, c_values, factor, local):
    rows, cols = local.shape
    members = sources.shape[0]
    return pl.pallas_call(
        carry_kernel,
        out_shape=jax.ShapeDtypeStruct((rows, cols), jnp.bfloat16),
        in_specs=[SCALARS, HBM, WHOLE, HBM, HBM],
        out_specs=HBM,
        scratch_shapes=[
            pltpu.VMEM((members * SP,) + incoming.shape[1:], incoming.dtype),
            pltpu.VMEM((rows, cols), jnp.float32),
            pltpu.VMEM((rows, cols), jnp.float32),
            pltpu.VMEM((rows, cols), jnp.bfloat16),
            pltpu.SemaphoreType.DMA((members, 3)),
            pltpu.SemaphoreType.DMA((members,)),
        ],
        compiler_params=pltpu.CompilerParams(vmem_limit_bytes=VMEM),
        cost_estimate=pl.CostEstimate(
            flops=2 * rows * NST * cols, bytes_accessed=8 * rows * cols, transcendentals=0
        ),
        name="carry_state",
    )(sources, incoming, c_values, factor, local)


CHUNK = 8


def attend_kernel(sources, prefix, queries, fresh, live, incoming, out, stacked, held, top, total, sems):
    members, slots = sources.shape
    heads = queries.shape[1] // HD
    factor = math.log2(math.e) / math.sqrt(HD)
    nothing = -1e30

    def copy(member, slot):
        return pltpu.make_async_copy(
            incoming.at[sources[member, slot]],
            held.at[member, pl.ds(pl.multiple_of(slot * PAGE, PAGE), PAGE), :],
            sems.at[member, slot],
        )

    for member in range(members):

        def start(slot, carry):
            @pl.when(slot < prefix[member])
            def _():
                copy(member, slot).start()

            @pl.when(slot >= prefix[member])
            def _():
                held[member, pl.ds(pl.multiple_of(slot * PAGE, PAGE), PAGE), :] = jnp.zeros(
                    (PAGE, 2 * HD), held.dtype
                )

            return carry

        lax.fori_loop(0, slots, start, 0)

    wide = CHUNK * PAGE
    block = 2 * PAGE
    causal = lax.broadcasted_iota(jnp.int32, (block, PAGE), 0) % PAGE >= lax.broadcasted_iota(
        jnp.int32, (block, PAGE), 1
    )
    for member in range(members):
        rows = slice(member * PAGE, (member + 1) * PAGE)
        for head in range(heads):
            stacked[head * PAGE : (head + 1) * PAGE, :] = queries[rows, head * HD : (head + 1) * HD]
        new_keys = fresh[rows, :HD]
        new_values = jnp.concatenate([jnp.ones((PAGE, HD), jnp.bfloat16), fresh[rows, HD:]], axis=1)
        for part in range(heads // 2):
            at = slice(part * block, (part + 1) * block)
            scores = lax.dot_general(
                stacked[at, :], new_keys, (((1,), (1,)), ((), ())), preferred_element_type=jnp.float32
            )
            scores = jnp.where(causal, scores * factor, nothing)
            best = jnp.max(scores, axis=1, keepdims=True)
            weights = jnp.exp2(scores - best).astype(jnp.bfloat16)
            top[at, :] = jnp.broadcast_to(best, (block, HD))
            total[at, :] = jnp.dot(weights, new_values, preferred_element_type=jnp.float32)

        def chunk(index, carry):
            base = index * CHUNK

            def finish(slot, inside):
                @pl.when(base + slot < prefix[member])
                def _():
                    copy(member, base + slot).wait()

                return inside

            lax.fori_loop(0, CHUNK, finish, 0)
            span = pl.ds(pl.multiple_of(index * wide, wide), wide)
            keys = held[member, span, :HD]
            values = jnp.concatenate([jnp.ones((wide, HD), jnp.bfloat16), held[member, span, HD:]], axis=1)
            seen = index * wide + lax.broadcasted_iota(jnp.int32, (1, wide), 1) < prefix[member] * PAGE
            bias = jnp.where(seen, 0.0, nothing)
            for part in range(heads // 2):
                at = slice(part * block, (part + 1) * block)
                scores = lax.dot_general(
                    stacked[at, :], keys, (((1,), (1,)), ((), ())), preferred_element_type=jnp.float32
                )
                scores = scores * factor + bias
                before = top[at, :1]
                best = jnp.maximum(before, jnp.max(scores, axis=1, keepdims=True))
                weights = jnp.exp2(scores - best).astype(jnp.bfloat16)
                shrink = jnp.exp2(before - best)
                top[at, :] = jnp.broadcast_to(best, (block, HD))
                total[at, :] = total[at, :] * shrink + jnp.dot(
                    weights, values, preferred_element_type=jnp.float32
                )
            return carry

        lax.fori_loop(0, (prefix[member] + CHUNK - 1) // CHUNK, chunk, 0)
        for head in range(heads):
            at = slice(head * PAGE, (head + 1) * PAGE)
            mixed = total[at, HD:] / total[at, :HD] * live[rows, :]
            out[rows, head * HD : (head + 1) * HD] = mixed.astype(jnp.bfloat16)


def attend(sources, prefix, queries, fresh, live, incoming):
    rows, cols = queries.shape
    members, slots = sources.shape
    heads = cols // HD
    return pl.pallas_call(
        attend_kernel,
        out_shape=jax.ShapeDtypeStruct((rows, cols), jnp.bfloat16),
        in_specs=[SCALARS, SCALARS] + [WHOLE] * 3 + [HBM],
        out_specs=WHOLE,
        scratch_shapes=[
            pltpu.VMEM((heads * PAGE, HD), jnp.bfloat16),
            pltpu.VMEM((members, slots * PAGE, 2 * HD), jnp.bfloat16),
            pltpu.VMEM((heads * PAGE, HD), jnp.float32),
            pltpu.VMEM((heads * PAGE, 2 * HD), jnp.float32),
            pltpu.SemaphoreType.DMA((members, slots)),
        ],
        compiler_params=pltpu.CompilerParams(vmem_limit_bytes=VMEM),
        cost_estimate=pl.CostEstimate(
            flops=280 * rows * cols * slots * PAGE,
            bytes_accessed=members * slots * PAGE * 4 * HD,
            transcendentals=rows * heads * slots * PAGE,
        ),
        name="attend",
    )(sources, prefix, queries, fresh, live, incoming)


def gather_tokens(tokens):
    middle = tokens.shape[0] // 2
    up, down = around_x(tokens, 1), around_x(tokens, -1)
    return [tokens, up, down, around_x(up[:middle], 1), around_x(down[middle:], -1)]


def body(
    tokens,
    x_weight,
    bc_weight,
    step_weight,
    step_bias,
    decay_log,
    skip_gain,
    queries,
    new_keyvals,
    page_pool,
    page_table,
    prefix_pages,
    new_counts,
):
    owners = lax.axis_size(DP)
    x = lax.axis_index("tensor")
    seq_dev = page_table.shape[0]
    pool_size = page_pool.shape[0]
    rows = tokens.shape[0]
    length = rows // seq_dev
    heads = step_bias.shape[0]

    sources = page_table // pool_size
    places = page_table % pool_size
    names = jnp.arange(owners, dtype=jnp.int32)[:, None]

    def wanted(part):
        asked = sources[:, part].reshape(1, -1) == names
        return jnp.max(jnp.where(asked, places[:, part].reshape(1, -1), 0), axis=1)

    asks = jnp.stack([wanted(slice(SP, None)), wanted(slice(0, SP))], axis=1)
    asks = jnp.pad(asks, ((0, 0), (0, 126))).reshape(owners, 1, 128)
    extra = bc_weight.shape[1]
    x_weight, bc_weight, step_weight, asks = lax.optimization_barrier(
        (x_weight, bc_weight, step_weight, asks)
    )
    step_wide = jnp.pad(step_weight, ((0, 0), (0, extra - heads)))
    weights = jnp.concatenate([x_weight, bc_weight, step_wide], axis=1)
    weights = lax.all_gather(weights, "z", axis=0)
    picks = lax.all_to_all(asks, DP, split_axis=0, concat_axis=0, tiled=True)
    kv_out = pack_pages(picks, 0, page_pool, 0)
    kv_in = lax.all_to_all(kv_out, DP, split_axis=0, concat_axis=0, tiled=True)
    later_pool, _, weights = lax.optimization_barrier((page_pool, kv_out, weights))
    state_out = pack_pages(picks, 1, later_pool, 100)
    state_in = lax.all_to_all(state_out, DP, split_axis=0, concat_axis=0, tiled=True)

    weights, _ = lax.optimization_barrier((weights, state_out))
    weights = lax.all_gather(weights, ("y", "core"), axis=0)
    weights = weights.reshape((NY, 2) + weights.shape[1:])
    tokens, _ = lax.optimization_barrier((tokens, kv_in))
    inner, extras = project(
        x.reshape(1).astype(jnp.int32), weights, gather_tokens(tokens), rows, 2 * extra
    )
    columns = extras[:, :extra].astype(jnp.bfloat16)
    step_raw = extras[:, extra : extra + heads]
    around = jnp.stack([columns] + [around_x(columns, -k) for k in range(1, NX)])
    quarters = [lax.dynamic_index_in_dim(around, (t - x) % NX, 0, keepdims=False) for t in range(NX)]
    b_values = jnp.concatenate(quarters[:2], axis=1)
    c_values = jnp.concatenate(quarters[2:], axis=1)

    live = (jnp.arange(length)[None, :] < new_counts[:, None]).astype(jnp.float32)
    step = jax.nn.softplus(step_raw + step_bias[None, :]).reshape(seq_dev, length, heads)
    step = step * live[:, :, None]
    decay = jnp.cumsum(-step * jnp.exp(decay_log)[None, None, :], axis=1)
    gain = jnp.repeat(skip_gain, HP)[None, :]
    live_column = live.reshape(rows, 1)
    local, factor = mix_locally(
        inner, b_values, c_values, decay, decay.transpose(0, 2, 1), step.transpose(0, 2, 1), gain, live_column
    )
    attention_out = attend(
        sources[:, SP:], prefix_pages, queries, new_keyvals, live_column, kv_in
    )
    mamba_out = carry_state(sources[:, :SP], state_in, c_values, factor, local)
    return (mamba_out, attention_out)


def solution(mesh):
    split = Mesh(mesh.devices.reshape(NY, NZ, 2, NX), DP + ("tensor",))
    placed = (
        P(DP, "tensor"),
        P(DP, "tensor"),
        P(DP, "tensor"),
        P(DP, "tensor"),
        P("tensor"),
        P("tensor"),
        P("tensor"),
        P(DP, "tensor"),
        P(DP, "tensor"),
        P(DP, None, "tensor"),
        P(DP, None),
        P(DP),
        P(DP),
    )
    return jax.shard_map(
        body,
        mesh=split,
        in_specs=placed,
        out_specs=(P(DP, "tensor"), P(DP, "tensor")),
        check_vma=False,
    )
```

```python
import functools
import math

import jax
import jax.numpy as jnp
from jax import lax
from jax.experimental import pallas as pl
from jax.experimental.pallas import tpu as pltpu
from jax.sharding import Mesh
from jax.sharding import PartitionSpec as P

HP = 64
NST = 256
HD = 128
PAGE = 128
SP = 16
NY = 4
NZ = 8
NX = 4
TILE = 256
EARLY = 768
DP = ("y", "z", "core")
VMEM = 62 * 1024 * 1024
ANY = pl.BlockSpec(memory_space=pl.ANY)
HBM = pl.BlockSpec(memory_space=pltpu.HBM)
WHOLE = pl.BlockSpec(memory_space=pltpu.VMEM)
SCALARS = pl.BlockSpec(memory_space=pltpu.SMEM)


def around_x(array, by):
    return lax.ppermute(array, "tensor", [(i, (i + by) % NX) for i in range(NX)])


def pack_kernel(column, picks, pool, out, held, in_sems, out_sems):
    owners = out.shape[0]
    parts = in_sems.shape[0]
    span = owners // parts

    def fetch(r, part):
        pltpu.make_async_copy(pool.at[picks[r, 0, column]], held.at[r], in_sems.at[part]).start()
        return part

    def store(part):
        rows = pl.ds(part * span, span)
        return pltpu.make_async_copy(held.at[rows], out.at[rows], out_sems.at[part])

    for part in range(parts):
        lax.fori_loop(part * span, (part + 1) * span, fetch, part, unroll=8)
    for part in range(parts):
        rows = pl.ds(part * span, span)
        pltpu.make_async_copy(pool.at[pl.ds(0, span)], held.at[rows], in_sems.at[part]).wait()
        store(part).start()
    for part in range(parts):
        store(part).wait()


def pack_pages(picks, column, pool):
    owners = picks.shape[0]
    page = pool.shape[1:]
    return pl.pallas_call(
        functools.partial(pack_kernel, column),
        out_shape=jax.ShapeDtypeStruct((owners,) + page, pool.dtype),
        in_specs=[SCALARS, HBM],
        out_specs=HBM,
        scratch_shapes=[
            pltpu.VMEM((owners,) + page, pool.dtype),
            pltpu.SemaphoreType.DMA((4,)),
            pltpu.SemaphoreType.DMA((4,)),
        ],
        compiler_params=pltpu.CompilerParams(vmem_limit_bytes=VMEM),
        cost_estimate=pl.CostEstimate(
            flops=0, bytes_accessed=4 * owners * page[0] * page[1], transcendentals=0
        ),
        name="pack_pages",
    )(picks, pool)


def project_kernel(raw, x, weights, *refs):
    pieces = refs[:5]
    outs = refs[5 : 6 + raw]
    w_all, t_all, w_sems, t_sems = refs[6 + raw :]
    tiles, wide = w_all.shape[0], w_all.shape[5]
    depth = t_all.shape[1]
    cols = pieces[0].shape[1]
    middle = pieces[3].shape[0]

    def columns(n):
        along = pl.ds(pl.multiple_of(n * wide, wide), wide)
        return [
            pltpu.make_async_copy(
                weights.at[y, core, :, :, along], w_all.at[n, y, :, core], w_sems.at[n, 2 * y + core]
            )
            for y in range(NY)
            for core in range(2)
        ]

    def start(n, carry):
        for copy in columns(n):
            copy.start()
        return carry

    copies = []
    for i, (first, by) in enumerate(((0, 0), (0, NX - 1), (0, 1), (0, 2), (middle, 2))):
        along = pl.multiple_of((x[0] + by) % NX * cols, cols)
        rows = pieces[i].shape[0]
        copies.append(
            pltpu.make_async_copy(
                pieces[i], t_all.at[pl.ds(first, rows), pl.ds(along, cols)], t_sems.at[i]
            )
        )
    for copy in copies:
        copy.start()
    lax.fori_loop(0, tiles, start, 0)
    for copy in copies:
        copy.wait()

    def product(n):
        for copy in columns(n):
            copy.wait()
        tile = w_all[n].reshape(depth, wide)
        return jnp.dot(t_all[...], tile, preferred_element_type=jnp.float32)

    def gated(n, carry):
        total = product(n)
        value = total / (1.0 + jnp.exp(-total))
        outs[0][:, pl.ds(pl.multiple_of(n * wide, wide), wide)] = value.astype(jnp.bfloat16)
        return carry

    lax.fori_loop(0, tiles - raw, gated, 0)
    if raw:
        outs[1][...] = product(tiles - 1)


def project(x, weights, pieces, rows, raw):
    cols = weights.shape[-1]
    depth = weights.size // cols
    shapes = [jax.ShapeDtypeStruct((rows, cols - raw * TILE), jnp.bfloat16)]
    if raw:
        shapes.append(jax.ShapeDtypeStruct((rows, TILE), jnp.float32))
    return pl.pallas_call(
        functools.partial(project_kernel, raw),
        out_shape=tuple(shapes),
        in_specs=[SCALARS, HBM] + [ANY] * 5,
        out_specs=(WHOLE,) * len(shapes),
        scratch_shapes=[
            pltpu.VMEM((cols // TILE, NY, NZ, 2, depth // (2 * NY * NZ), TILE), jnp.bfloat16),
            pltpu.VMEM((rows, depth), jnp.bfloat16),
            pltpu.SemaphoreType.DMA((cols // TILE, 2 * NY)),
            pltpu.SemaphoreType.DMA((5,)),
        ],
        compiler_params=pltpu.CompilerParams(vmem_limit_bytes=VMEM),
        cost_estimate=pl.CostEstimate(
            flops=2 * rows * depth * cols, bytes_accessed=2 * depth * (cols + rows), transcendentals=rows * cols
        ),
        name="project",
    )(x, weights, *pieces)


def split_dot(left, right):
    high = left.astype(jnp.bfloat16)
    low = (left - high.astype(jnp.float32)).astype(jnp.bfloat16)
    return jnp.dot(high, right, preferred_element_type=jnp.float32) + jnp.dot(
        low, right, preferred_element_type=jnp.float32
    )


def local_kernel(inner_a, inner_b, b_values, c_values, decay, decay_t, step_t, gain, live, out, factor):
    length = PAGE
    row = lax.broadcasted_iota(jnp.int32, (length, length), 0)
    column = lax.broadcasted_iota(jnp.int32, (length, length), 1)
    causal = row >= column
    first = lax.broadcasted_iota(jnp.int32, (length, 2 * HP), 1) < HP
    for member in range(decay.shape[0]):
        rows = slice(member * length, (member + 1) * length)
        crossing = lax.dot_general(
            c_values[rows, :],
            b_values[rows, :],
            (((1,), (1,)), ((), ())),
            preferred_element_type=jnp.float32,
        )
        fades = jnp.exp(decay[member])
        for pair in range(decay.shape[2] // 2):
            lanes = slice(pair * 2 * HP, (pair + 1) * 2 * HP)
            if pair * 2 * HP < EARLY:
                values = inner_a[rows, lanes]
            else:
                values = inner_b[rows, pair * 2 * HP - EARLY : (pair + 1) * 2 * HP - EARLY]
            parts = []
            for head in (2 * pair, 2 * pair + 1):
                gaps = decay[member, :, head : head + 1] - decay_t[member, head : head + 1, :]
                gaps = jnp.where(causal, gaps, -jnp.inf)
                mixing = jnp.exp(gaps) * crossing * step_t[member, head : head + 1, :]
                parts.append(split_dot(mixing, values))
            local = jnp.where(first, parts[0], parts[1])
            local = local + gain[:, lanes] * values.astype(jnp.float32)
            out[rows, lanes] = local * live[rows, :]
            fade = jnp.where(first, fades[:, 2 * pair : 2 * pair + 1], fades[:, 2 * pair + 1 : 2 * pair + 2])
            factor[rows, lanes] = fade * live[rows, :]


def mix_locally(inner_a, inner_b, b_values, c_values, decay, decay_t, step_t, gain, live):
    rows, cols = inner_a.shape[0], gain.shape[1]
    return pl.pallas_call(
        local_kernel,
        out_shape=(jax.ShapeDtypeStruct((rows, cols), jnp.float32),) * 2,
        in_specs=[WHOLE] * 9,
        out_specs=(WHOLE,) * 2,
        compiler_params=pltpu.CompilerParams(vmem_limit_bytes=VMEM),
        cost_estimate=pl.CostEstimate(
            flops=8 * rows * PAGE * cols, bytes_accessed=6 * rows * cols, transcendentals=rows * PAGE * 32
        ),
        name="mix_locally",
    )(inner_a, inner_b, b_values, c_values, decay, decay_t, step_t, gain, live)


def carry_kernel(
    sources, incoming, c_values, factor, local, out, held, factors, locals_, ready, in_sems, out_sems
):
    members = sources.shape[0]
    span = 2 * PAGE

    def rows_of(member):
        return pl.ds(member * PAGE, PAGE)

    def bring(member):
        rows = rows_of(member)
        return [
            pltpu.make_async_copy(factor.at[rows, :], factors.at[rows, :], in_sems.at[member, 1]),
            pltpu.make_async_copy(local.at[rows, :], locals_.at[rows, :], in_sems.at[member, 2]),
        ]

    def store(member):
        rows = rows_of(member)
        return pltpu.make_async_copy(ready.at[rows, :], out.at[rows, :], out_sems.at[member])

    for member in range(members):
        for page in range(SP):
            pltpu.make_async_copy(
                incoming.at[sources[member, page]], held.at[member * SP + page], in_sems.at[member, 0]
            ).start()
        for copy in bring(member):
            copy.start()
    for member in range(members):
        rows = rows_of(member)
        pages = pl.ds(member * SP, SP)
        pltpu.make_async_copy(incoming.at[pl.ds(0, SP)], held.at[pages], in_sems.at[member, 0]).wait()
        for copy in bring(member):
            copy.wait()
        for page in range(0, SP, 2):
            lanes = slice(page * 2 * HP, page * 2 * HP + span)
            pair = held[member * SP + page : member * SP + page + 2].reshape(span, NST)
            carried = lax.dot_general(
                c_values[rows, :], pair, (((1,), (1,)), ((), ())), preferred_element_type=jnp.float32
            )
            total = locals_[rows, lanes] + carried * factors[rows, lanes]
            ready[rows, lanes] = total.astype(jnp.bfloat16)
        store(member).start()
    for member in range(members):
        store(member).wait()


def carry_state(sources, incoming, c_values, factor, local):
    rows, cols = local.shape
    members = sources.shape[0]
    return pl.pallas_call(
        carry_kernel,
        out_shape=jax.ShapeDtypeStruct((rows, cols), jnp.bfloat16),
        in_specs=[SCALARS, HBM, WHOLE, HBM, HBM],
        out_specs=HBM,
        scratch_shapes=[
            pltpu.VMEM((members * SP,) + incoming.shape[1:], incoming.dtype),
            pltpu.VMEM((rows, cols), jnp.float32),
            pltpu.VMEM((rows, cols), jnp.float32),
            pltpu.VMEM((rows, cols), jnp.bfloat16),
            pltpu.SemaphoreType.DMA((members, 3)),
            pltpu.SemaphoreType.DMA((members,)),
        ],
        compiler_params=pltpu.CompilerParams(vmem_limit_bytes=VMEM),
        cost_estimate=pl.CostEstimate(
            flops=2 * rows * NST * cols, bytes_accessed=8 * rows * cols, transcendentals=0
        ),
        name="carry_state",
    )(sources, incoming, c_values, factor, local)


CHUNK = 8


def attend_kernel(sources, prefix, queries, fresh, live, incoming, out, stacked, held, top, total, sems):
    members, slots = sources.shape
    heads = queries.shape[1] // HD
    factor = math.log2(math.e) / math.sqrt(HD)
    nothing = -1e30

    def copy(member, slot):
        return pltpu.make_async_copy(
            incoming.at[sources[member, slot]],
            held.at[member, pl.ds(pl.multiple_of(slot * PAGE, PAGE), PAGE), :],
            sems.at[member, slot],
        )

    for member in range(members):

        def start(slot, carry):
            @pl.when(slot < prefix[member])
            def _():
                copy(member, slot).start()

            @pl.when(slot >= prefix[member])
            def _():
                held[member, pl.ds(pl.multiple_of(slot * PAGE, PAGE), PAGE), :] = jnp.zeros(
                    (PAGE, 2 * HD), held.dtype
                )

            return carry

        lax.fori_loop(0, slots, start, 0)

    wide = CHUNK * PAGE
    block = 2 * PAGE
    causal = lax.broadcasted_iota(jnp.int32, (block, PAGE), 0) % PAGE >= lax.broadcasted_iota(
        jnp.int32, (block, PAGE), 1
    )
    for member in range(members):
        rows = slice(member * PAGE, (member + 1) * PAGE)
        for head in range(heads):
            stacked[head * PAGE : (head + 1) * PAGE, :] = queries[rows, head * HD : (head + 1) * HD]
        new_keys = fresh[rows, :HD]
        new_values = jnp.concatenate([jnp.ones((PAGE, HD), jnp.bfloat16), fresh[rows, HD:]], axis=1)
        for part in range(heads // 2):
            at = slice(part * block, (part + 1) * block)
            scores = lax.dot_general(
                stacked[at, :], new_keys, (((1,), (1,)), ((), ())), preferred_element_type=jnp.float32
            )
            scores = jnp.where(causal, scores * factor, nothing)
            best = jnp.max(scores, axis=1, keepdims=True)
            weights = jnp.exp2(scores - best).astype(jnp.bfloat16)
            top[at, :] = jnp.broadcast_to(best, (block, HD))
            total[at, :] = jnp.dot(weights, new_values, preferred_element_type=jnp.float32)

        def chunk(index, carry):
            base = index * CHUNK

            def finish(slot, inside):
                @pl.when(base + slot < prefix[member])
                def _():
                    copy(member, base + slot).wait()

                return inside

            lax.fori_loop(0, CHUNK, finish, 0)
            span = pl.ds(pl.multiple_of(index * wide, wide), wide)
            keys = held[member, span, :HD]
            values = jnp.concatenate([jnp.ones((wide, HD), jnp.bfloat16), held[member, span, HD:]], axis=1)
            seen = index * wide + lax.broadcasted_iota(jnp.int32, (1, wide), 1) < prefix[member] * PAGE
            bias = jnp.where(seen, 0.0, nothing)
            for part in range(heads // 2):
                at = slice(part * block, (part + 1) * block)
                scores = lax.dot_general(
                    stacked[at, :], keys, (((1,), (1,)), ((), ())), preferred_element_type=jnp.float32
                )
                scores = scores * factor + bias
                before = top[at, :1]
                best = jnp.maximum(before, jnp.max(scores, axis=1, keepdims=True))
                weights = jnp.exp2(scores - best).astype(jnp.bfloat16)
                shrink = jnp.exp2(before - best)
                top[at, :] = jnp.broadcast_to(best, (block, HD))
                total[at, :] = total[at, :] * shrink + jnp.dot(
                    weights, values, preferred_element_type=jnp.float32
                )
            return carry

        lax.fori_loop(0, (prefix[member] + CHUNK - 1) // CHUNK, chunk, 0)
        for head in range(heads):
            at = slice(head * PAGE, (head + 1) * PAGE)
            mixed = total[at, HD:] / total[at, :HD] * live[rows, :]
            out[rows, head * HD : (head + 1) * HD] = mixed.astype(jnp.bfloat16)


def attend(sources, prefix, queries, fresh, live, incoming):
    rows, cols = queries.shape
    members, slots = sources.shape
    heads = cols // HD
    return pl.pallas_call(
        attend_kernel,
        out_shape=jax.ShapeDtypeStruct((rows, cols), jnp.bfloat16),
        in_specs=[SCALARS, SCALARS] + [WHOLE] * 3 + [HBM],
        out_specs=WHOLE,
        scratch_shapes=[
            pltpu.VMEM((heads * PAGE, HD), jnp.bfloat16),
            pltpu.VMEM((members, slots * PAGE, 2 * HD), jnp.bfloat16),
            pltpu.VMEM((heads * PAGE, HD), jnp.float32),
            pltpu.VMEM((heads * PAGE, 2 * HD), jnp.float32),
            pltpu.SemaphoreType.DMA((members, slots)),
        ],
        compiler_params=pltpu.CompilerParams(vmem_limit_bytes=VMEM),
        cost_estimate=pl.CostEstimate(
            flops=4 * rows * cols * slots * PAGE,
            bytes_accessed=members * slots * PAGE * 4 * HD,
            transcendentals=rows * heads * slots * PAGE,
        ),
        name="attend",
    )(sources, prefix, queries, fresh, live, incoming)


def gather_tokens(tokens):
    middle = tokens.shape[0] // 2
    up, down = around_x(tokens, 1), around_x(tokens, -1)
    return [tokens, up, down, around_x(up[:middle], 1), around_x(down[middle:], -1)]


def body(
    tokens,
    x_weight,
    bc_weight,
    step_weight,
    step_bias,
    decay_log,
    skip_gain,
    queries,
    new_keyvals,
    page_pool,
    page_table,
    prefix_pages,
    new_counts,
):
    owners = lax.axis_size(DP)
    x = lax.axis_index("tensor")
    seq_dev = page_table.shape[0]
    pool_size = page_pool.shape[0]
    rows = tokens.shape[0]
    length = rows // seq_dev
    heads = step_bias.shape[0]

    sources = page_table // pool_size
    places = page_table % pool_size
    names = jnp.arange(owners, dtype=jnp.int32)[:, None]

    def wanted(part):
        asked = sources[:, part].reshape(1, -1) == names
        return jnp.max(jnp.where(asked, places[:, part].reshape(1, -1), 0), axis=1)

    asks = jnp.stack([wanted(slice(SP, None)), wanted(slice(0, SP))], axis=1)
    asks = jnp.pad(asks, ((0, 0), (0, 126))).reshape(owners, 1, 128)
    extra = bc_weight.shape[1]
    x_weight, bc_weight, step_weight, asks = lax.optimization_barrier(
        (x_weight, bc_weight, step_weight, asks)
    )
    step_wide = jnp.pad(step_weight, ((0, 0), (0, extra - heads)))
    part_a = jnp.concatenate([x_weight[:, :EARLY], bc_weight, step_wide], axis=1)
    part_a = lax.all_gather(part_a, "z", axis=0)
    part_b = lax.all_gather(x_weight[:, EARLY:], "z", axis=0)
    picks = lax.all_to_all(asks, DP, split_axis=0, concat_axis=0, tiled=True)
    kv_out = pack_pages(picks, 0, page_pool)
    kv_in = lax.all_to_all(kv_out, DP, split_axis=0, concat_axis=0, tiled=True)
    later_pool, _ = lax.optimization_barrier((page_pool, kv_out))
    state_out = pack_pages(picks, 1, later_pool)
    state_in = lax.all_to_all(state_out, DP, split_axis=0, concat_axis=0, tiled=True)

    part_a, _ = lax.optimization_barrier((part_a, kv_out))
    part_a = lax.all_gather(part_a, ("y", "core"), axis=0)
    part_b, tokens, _, _ = lax.optimization_barrier((part_b, tokens, kv_in, state_out))
    part_b = lax.all_gather(part_b, ("y", "core"), axis=0)
    pieces = gather_tokens(tokens)
    at = x.reshape(1).astype(jnp.int32)
    inner_a, extras = project(at, part_a.reshape((NY, 2) + part_a.shape[1:]), pieces, rows, 1)
    (inner_b,) = project(at, part_b.reshape((NY, 2) + part_b.shape[1:]), pieces, rows, 0)
    columns = extras[:, :extra].astype(jnp.bfloat16)
    step_raw = extras[:, extra : extra + heads]
    around = jnp.stack([columns] + [around_x(columns, -k) for k in range(1, NX)])
    quarters = [lax.dynamic_index_in_dim(around, (t - x) % NX, 0, keepdims=False) for t in range(NX)]
    b_values = jnp.concatenate(quarters[:2], axis=1)
    c_values = jnp.concatenate(quarters[2:], axis=1)

    live = (jnp.arange(length)[None, :] < new_counts[:, None]).astype(jnp.float32)
    step = jax.nn.softplus(step_raw + step_bias[None, :]).reshape(seq_dev, length, heads)
    step = step * live[:, :, None]
    decay = jnp.cumsum(-step * jnp.exp(decay_log)[None, None, :], axis=1)
    gain = jnp.repeat(skip_gain, HP)[None, :]
    live_column = live.reshape(rows, 1)
    local, factor = mix_locally(
        inner_a, inner_b, b_values, c_values, decay, decay.transpose(0, 2, 1), step.transpose(0, 2, 1), gain, live_column
    )
    attention_out = attend(
        sources[:, SP:], prefix_pages, queries, new_keyvals, live_column, kv_in
    )
    mamba_out = carry_state(sources[:, :SP], state_in, c_values, factor, local)
    return (mamba_out, attention_out)


def solution(mesh):
    split = Mesh(mesh.devices.reshape(NY, NZ, 2, NX), DP + ("tensor",))
    placed = (
        P(DP, "tensor"),
        P(DP, "tensor"),
        P(DP, "tensor"),
        P(DP, "tensor"),
        P("tensor"),
        P("tensor"),
        P("tensor"),
        P(DP, "tensor"),
        P(DP, "tensor"),
        P(DP, None, "tensor"),
        P(DP, None),
        P(DP),
        P(DP),
    )
    return jax.shard_map(
        body,
        mesh=split,
        in_specs=placed,
        out_specs=(P(DP, "tensor"), P(DP, "tensor")),
        check_vma=False,
    )
```

```python
import functools
import math

import jax
import jax.numpy as jnp
from jax import lax
from jax.experimental import pallas as pl
from jax.experimental.pallas import tpu as pltpu
from jax.sharding import Mesh
from jax.sharding import PartitionSpec as P

HP = 64
NST = 256
HD = 128
PAGE = 128
SP = 16
NY = 4
NZ = 8
NX = 4
DP = ("y", "z", "core")
VMEM = 62 * 1024 * 1024
PASS_COST = 840 * 1024 * 1024
ANY = pl.BlockSpec(memory_space=pl.ANY)
HBM = pl.BlockSpec(memory_space=pltpu.HBM)
WHOLE = pl.BlockSpec(memory_space=pltpu.VMEM)
SCALARS = pl.BlockSpec(memory_space=pltpu.SMEM)


def around_x(array, by):
    return lax.ppermute(array, "tensor", [(i, (i + by) % NX) for i in range(NX)])


def pack_kernel(column, picks, pool, out, held, in_sems, out_sems):
    owners = out.shape[0]
    parts = in_sems.shape[0]
    span = owners // parts

    def fetch(r, part):
        pltpu.make_async_copy(pool.at[picks[r, 0, column]], held.at[r], in_sems.at[part]).start()
        return part

    def store(part):
        rows = pl.ds(part * span, span)
        return pltpu.make_async_copy(held.at[rows], out.at[rows], out_sems.at[part])

    for part in range(parts):
        lax.fori_loop(part * span, (part + 1) * span, fetch, part, unroll=8)
    for part in range(parts):
        rows = pl.ds(part * span, span)
        pltpu.make_async_copy(pool.at[pl.ds(0, span)], held.at[rows], in_sems.at[part]).wait()
        store(part).start()
    for part in range(parts):
        store(part).wait()


def pack_pages(picks, column, pool):
    owners = picks.shape[0]
    page = pool.shape[1:]
    return pl.pallas_call(
        functools.partial(pack_kernel, column),
        out_shape=jax.ShapeDtypeStruct((owners,) + page, pool.dtype),
        in_specs=[SCALARS, HBM],
        out_specs=HBM,
        scratch_shapes=[
            pltpu.VMEM((owners,) + page, pool.dtype),
            pltpu.SemaphoreType.DMA((4,)),
            pltpu.SemaphoreType.DMA((4,)),
        ],
        compiler_params=pltpu.CompilerParams(vmem_limit_bytes=VMEM),
        cost_estimate=pl.CostEstimate(
            flops=0, bytes_accessed=4 * owners * page[0] * page[1], transcendentals=0
        ),
        name="pack_pages",
    )(picks, pool)


def pass_kernel(weights, out):
    pass


def pass_on(weights):
    return pl.pallas_call(
        pass_kernel,
        out_shape=jax.ShapeDtypeStruct(weights.shape, weights.dtype),
        in_specs=[HBM],
        out_specs=HBM,
        input_output_aliases={0: 0},
        compiler_params=pltpu.CompilerParams(vmem_limit_bytes=VMEM),
        cost_estimate=pl.CostEstimate(flops=0, bytes_accessed=PASS_COST, transcendentals=0),
        name="pass_on",
    )(weights)


def project_kernel(x, weights, *refs):
    pieces = refs[:5]
    main_out, extra_out, w_all, t_all, w_sems, t_sems = refs[5:]
    tiles, wide = w_all.shape[0], w_all.shape[5]
    depth = t_all.shape[1]
    cols = pieces[0].shape[1]
    middle = pieces[3].shape[0]

    def columns(n):
        along = pl.ds(pl.multiple_of(n * wide, wide), wide)
        return [
            pltpu.make_async_copy(
                weights.at[y, core, :, :, along], w_all.at[n, y, :, core], w_sems.at[n, 2 * y + core]
            )
            for y in range(NY)
            for core in range(2)
        ]

    def start(n, carry):
        for copy in columns(n):
            copy.start()
        return carry

    copies = []
    for i, (first, by) in enumerate(((0, 0), (0, NX - 1), (0, 1), (0, 2), (middle, 2))):
        along = pl.multiple_of((x[0] + by) % NX * cols, cols)
        rows = pieces[i].shape[0]
        copies.append(
            pltpu.make_async_copy(
                pieces[i], t_all.at[pl.ds(first, rows), pl.ds(along, cols)], t_sems.at[i]
            )
        )
    for copy in copies:
        copy.start()
    lax.fori_loop(0, tiles, start, 0)
    for copy in copies:
        copy.wait()

    def product(n):
        for copy in columns(n):
            copy.wait()
        tile = w_all[n].reshape(depth, wide)
        return jnp.dot(t_all[...], tile, preferred_element_type=jnp.float32)

    def main_tile(n, carry):
        total = product(n)
        value = total / (1.0 + jnp.exp(-total))
        main_out[:, pl.ds(pl.multiple_of(n * wide, wide), wide)] = value.astype(jnp.bfloat16)
        return carry

    lax.fori_loop(0, tiles - 1, main_tile, 0)
    extra_out[...] = product(tiles - 1)


def project(x, weights, pieces, rows, wide):
    cols = weights.shape[-1]
    depth = weights.size // cols
    main = cols - wide
    return pl.pallas_call(
        project_kernel,
        out_shape=(
            jax.ShapeDtypeStruct((rows, main), jnp.bfloat16),
            jax.ShapeDtypeStruct((rows, wide), jnp.float32),
        ),
        in_specs=[SCALARS, HBM] + [ANY] * 5,
        out_specs=(WHOLE,) * 2,
        scratch_shapes=[
            pltpu.VMEM((cols // wide, NY, NZ, 2, depth // (2 * NY * NZ), wide), jnp.bfloat16),
            pltpu.VMEM((rows, depth), jnp.bfloat16),
            pltpu.SemaphoreType.DMA((cols // wide, 2 * NY)),
            pltpu.SemaphoreType.DMA((5,)),
        ],
        compiler_params=pltpu.CompilerParams(vmem_limit_bytes=VMEM),
        cost_estimate=pl.CostEstimate(
            flops=2 * rows * depth * cols, bytes_accessed=2 * depth * (cols + rows), transcendentals=rows * main
        ),
        name="project",
    )(x, weights, *pieces)


def split_dot(left, right):
    high = left.astype(jnp.bfloat16)
    low = (left - high.astype(jnp.float32)).astype(jnp.bfloat16)
    return jnp.dot(high, right, preferred_element_type=jnp.float32) + jnp.dot(
        low, right, preferred_element_type=jnp.float32
    )


def local_kernel(inner, b_values, c_values, decay, decay_t, step_t, gain, live, out, factor):
    length = PAGE
    row = lax.broadcasted_iota(jnp.int32, (length, length), 0)
    column = lax.broadcasted_iota(jnp.int32, (length, length), 1)
    causal = row >= column
    first = lax.broadcasted_iota(jnp.int32, (length, 2 * HP), 1) < HP
    for member in range(decay.shape[0]):
        rows = slice(member * length, (member + 1) * length)
        crossing = lax.dot_general(
            c_values[rows, :],
            b_values[rows, :],
            (((1,), (1,)), ((), ())),
            preferred_element_type=jnp.float32,
        )
        fades = jnp.exp(decay[member])
        for pair in range(decay.shape[2] // 2):
            lanes = slice(pair * 2 * HP, (pair + 1) * 2 * HP)
            values = inner[rows, lanes]
            parts = []
            for head in (2 * pair, 2 * pair + 1):
                gaps = decay[member, :, head : head + 1] - decay_t[member, head : head + 1, :]
                gaps = jnp.where(causal, gaps, -jnp.inf)
                mixing = jnp.exp(gaps) * crossing * step_t[member, head : head + 1, :]
                parts.append(split_dot(mixing, values))
            local = jnp.where(first, parts[0], parts[1])
            local = local + gain[:, lanes] * values.astype(jnp.float32)
            out[rows, lanes] = local * live[rows, :]
            fade = jnp.where(first, fades[:, 2 * pair : 2 * pair + 1], fades[:, 2 * pair + 1 : 2 * pair + 2])
            factor[rows, lanes] = fade * live[rows, :]


def mix_locally(inner, b_values, c_values, decay, decay_t, step_t, gain, live):
    rows, cols = inner.shape
    return pl.pallas_call(
        local_kernel,
        out_shape=(jax.ShapeDtypeStruct((rows, cols), jnp.float32),) * 2,
        in_specs=[WHOLE] * 8,
        out_specs=(WHOLE,) * 2,
        compiler_params=pltpu.CompilerParams(vmem_limit_bytes=VMEM),
        cost_estimate=pl.CostEstimate(
            flops=8 * rows * PAGE * cols, bytes_accessed=6 * rows * cols, transcendentals=rows * PAGE * 32
        ),
        name="mix_locally",
    )(inner, b_values, c_values, decay, decay_t, step_t, gain, live)


def carry_kernel(
    sources, incoming, c_values, factor, local, out, held, factors, locals_, ready, in_sems, out_sems
):
    members = sources.shape[0]
    span = 2 * PAGE

    def rows_of(member):
        return pl.ds(member * PAGE, PAGE)

    def bring(member):
        rows = rows_of(member)
        return [
            pltpu.make_async_copy(factor.at[rows, :], factors.at[rows, :], in_sems.at[member, 1]),
            pltpu.make_async_copy(local.at[rows, :], locals_.at[rows, :], in_sems.at[member, 2]),
        ]

    def store(member):
        rows = rows_of(member)
        return pltpu.make_async_copy(ready.at[rows, :], out.at[rows, :], out_sems.at[member])

    for member in range(members):
        for page in range(SP):
            pltpu.make_async_copy(
                incoming.at[sources[member, page]], held.at[member * SP + page], in_sems.at[member, 0]
            ).start()
        for copy in bring(member):
            copy.start()
    for member in range(members):
        rows = rows_of(member)
        pages = pl.ds(member * SP, SP)
        pltpu.make_async_copy(incoming.at[pl.ds(0, SP)], held.at[pages], in_sems.at[member, 0]).wait()
        for copy in bring(member):
            copy.wait()
        for page in range(0, SP, 2):
            lanes = slice(page * 2 * HP, page * 2 * HP + span)
            pair = held[member * SP + page : member * SP + page + 2].reshape(span, NST)
            carried = lax.dot_general(
                c_values[rows, :], pair, (((1,), (1,)), ((), ())), preferred_element_type=jnp.float32
            )
            total = locals_[rows, lanes] + carried * factors[rows, lanes]
            ready[rows, lanes] = total.astype(jnp.bfloat16)
        store(member).start()
    for member in range(members):
        store(member).wait()


def carry_state(sources, incoming, c_values, factor, local):
    rows, cols = local.shape
    members = sources.shape[0]
    return pl.pallas_call(
        carry_kernel,
        out_shape=jax.ShapeDtypeStruct((rows, cols), jnp.bfloat16),
        in_specs=[SCALARS, HBM, WHOLE, HBM, HBM],
        out_specs=HBM,
        scratch_shapes=[
            pltpu.VMEM((members * SP,) + incoming.shape[1:], incoming.dtype),
            pltpu.VMEM((rows, cols), jnp.float32),
            pltpu.VMEM((rows, cols), jnp.float32),
            pltpu.VMEM((rows, cols), jnp.bfloat16),
            pltpu.SemaphoreType.DMA((members, 3)),
            pltpu.SemaphoreType.DMA((members,)),
        ],
        compiler_params=pltpu.CompilerParams(vmem_limit_bytes=VMEM),
        cost_estimate=pl.CostEstimate(
            flops=2 * rows * NST * cols, bytes_accessed=8 * rows * cols, transcendentals=0
        ),
        name="carry_state",
    )(sources, incoming, c_values, factor, local)


CHUNK = 8


def attend_kernel(sources, prefix, queries, fresh, live, incoming, out, stacked, held, top, total, sems):
    members, slots = sources.shape
    heads = queries.shape[1] // HD
    factor = math.log2(math.e) / math.sqrt(HD)
    nothing = -1e30

    def copy(member, slot):
        return pltpu.make_async_copy(
            incoming.at[sources[member, slot]],
            held.at[member, pl.ds(pl.multiple_of(slot * PAGE, PAGE), PAGE), :],
            sems.at[member, slot],
        )

    for member in range(members):

        def start(slot, carry):
            @pl.when(slot < prefix[member])
            def _():
                copy(member, slot).start()

            @pl.when(slot >= prefix[member])
            def _():
                held[member, pl.ds(pl.multiple_of(slot * PAGE, PAGE), PAGE), :] = jnp.zeros(
                    (PAGE, 2 * HD), held.dtype
                )

            return carry

        lax.fori_loop(0, slots, start, 0)

    wide = CHUNK * PAGE
    block = 2 * PAGE
    causal = lax.broadcasted_iota(jnp.int32, (block, PAGE), 0) % PAGE >= lax.broadcasted_iota(
        jnp.int32, (block, PAGE), 1
    )
    for member in range(members):
        rows = slice(member * PAGE, (member + 1) * PAGE)
        for head in range(heads):
            stacked[head * PAGE : (head + 1) * PAGE, :] = queries[rows, head * HD : (head + 1) * HD]
        new_keys = fresh[rows, :HD]
        new_values = jnp.concatenate([jnp.ones((PAGE, HD), jnp.bfloat16), fresh[rows, HD:]], axis=1)
        for part in range(heads // 2):
            at = slice(part * block, (part + 1) * block)
            scores = lax.dot_general(
                stacked[at, :], new_keys, (((1,), (1,)), ((), ())), preferred_element_type=jnp.float32
            )
            scores = jnp.where(causal, scores * factor, nothing)
            best = jnp.max(scores, axis=1, keepdims=True)
            weights = jnp.exp2(scores - best).astype(jnp.bfloat16)
            top[at, :] = jnp.broadcast_to(best, (block, HD))
            total[at, :] = jnp.dot(weights, new_values, preferred_element_type=jnp.float32)

        def chunk(index, carry):
            base = index * CHUNK

            def finish(slot, inside):
                @pl.when(base + slot < prefix[member])
                def _():
                    copy(member, base + slot).wait()

                return inside

            lax.fori_loop(0, CHUNK, finish, 0)
            span = pl.ds(pl.multiple_of(index * wide, wide), wide)
            keys = held[member, span, :HD]
            values = jnp.concatenate([jnp.ones((wide, HD), jnp.bfloat16), held[member, span, HD:]], axis=1)
            seen = index * wide + lax.broadcasted_iota(jnp.int32, (1, wide), 1) < prefix[member] * PAGE
            bias = jnp.where(seen, 0.0, nothing)
            for part in range(heads // 2):
                at = slice(part * block, (part + 1) * block)
                scores = lax.dot_general(
                    stacked[at, :], keys, (((1,), (1,)), ((), ())), preferred_element_type=jnp.float32
                )
                scores = scores * factor + bias
                before = top[at, :1]
                best = jnp.maximum(before, jnp.max(scores, axis=1, keepdims=True))
                weights = jnp.exp2(scores - best).astype(jnp.bfloat16)
                shrink = jnp.exp2(before - best)
                top[at, :] = jnp.broadcast_to(best, (block, HD))
                total[at, :] = total[at, :] * shrink + jnp.dot(
                    weights, values, preferred_element_type=jnp.float32
                )
            return carry

        lax.fori_loop(0, (prefix[member] + CHUNK - 1) // CHUNK, chunk, 0)
        for head in range(heads):
            at = slice(head * PAGE, (head + 1) * PAGE)
            mixed = total[at, HD:] / total[at, :HD] * live[rows, :]
            out[rows, head * HD : (head + 1) * HD] = mixed.astype(jnp.bfloat16)


def attend(sources, prefix, queries, fresh, live, incoming):
    rows, cols = queries.shape
    members, slots = sources.shape
    heads = cols // HD
    return pl.pallas_call(
        attend_kernel,
        out_shape=jax.ShapeDtypeStruct((rows, cols), jnp.bfloat16),
        in_specs=[SCALARS, SCALARS] + [WHOLE] * 3 + [HBM],
        out_specs=WHOLE,
        scratch_shapes=[
            pltpu.VMEM((heads * PAGE, HD), jnp.bfloat16),
            pltpu.VMEM((members, slots * PAGE, 2 * HD), jnp.bfloat16),
            pltpu.VMEM((heads * PAGE, HD), jnp.float32),
            pltpu.VMEM((heads * PAGE, 2 * HD), jnp.float32),
            pltpu.SemaphoreType.DMA((members, slots)),
        ],
        compiler_params=pltpu.CompilerParams(vmem_limit_bytes=VMEM),
        cost_estimate=pl.CostEstimate(
            flops=272 * rows * cols * slots * PAGE,
            bytes_accessed=members * slots * PAGE * 4 * HD,
            transcendentals=rows * heads * slots * PAGE,
        ),
        name="attend",
    )(sources, prefix, queries, fresh, live, incoming)


def gather_tokens(tokens):
    middle = tokens.shape[0] // 2
    up, down = around_x(tokens, 1), around_x(tokens, -1)
    return [tokens, up, down, around_x(up[:middle], 1), around_x(down[middle:], -1)]


def body(
    tokens,
    x_weight,
    bc_weight,
    step_weight,
    step_bias,
    decay_log,
    skip_gain,
    queries,
    new_keyvals,
    page_pool,
    page_table,
    prefix_pages,
    new_counts,
):
    owners = lax.axis_size(DP)
    x = lax.axis_index("tensor")
    seq_dev = page_table.shape[0]
    pool_size = page_pool.shape[0]
    rows = tokens.shape[0]
    length = rows // seq_dev
    heads = step_bias.shape[0]

    sources = page_table // pool_size
    places = page_table % pool_size
    names = jnp.arange(owners, dtype=jnp.int32)[:, None]

    def wanted(part):
        asked = sources[:, part].reshape(1, -1) == names
        return jnp.max(jnp.where(asked, places[:, part].reshape(1, -1), 0), axis=1)

    asks = jnp.stack([wanted(slice(SP, None)), wanted(slice(0, SP))], axis=1)
    asks = jnp.pad(asks, ((0, 0), (0, 126))).reshape(owners, 1, 128)
    extra = bc_weight.shape[1]
    x_weight, bc_weight, step_weight, asks = lax.optimization_barrier(
        (x_weight, bc_weight, step_weight, asks)
    )
    step_wide = jnp.pad(step_weight, ((0, 0), (0, extra - heads)))
    weights = jnp.concatenate([x_weight, bc_weight, step_wide], axis=1)
    weights = lax.all_gather(weights, "z", axis=0)
    picks = lax.all_to_all(asks, DP, split_axis=0, concat_axis=0, tiled=True)
    kv_out = pack_pages(picks, 0, page_pool)
    state_out = pack_pages(picks, 1, page_pool)
    kv_out, state_out = lax.optimization_barrier((kv_out, state_out))
    kv_in = lax.all_to_all(kv_out, DP, split_axis=0, concat_axis=0, tiled=True)
    state_in = lax.all_to_all(state_out, DP, split_axis=0, concat_axis=0, tiled=True)

    weights, _ = lax.optimization_barrier((weights, state_out))
    weights = pass_on(weights)
    weights = lax.all_gather(weights, ("y", "core"), axis=0)
    weights = weights.reshape((NY, 2) + weights.shape[1:])
    tokens, _ = lax.optimization_barrier((tokens, kv_in))
    inner, extras = project(
        x.reshape(1).astype(jnp.int32), weights, gather_tokens(tokens), rows, 2 * extra
    )
    columns = extras[:, :extra].astype(jnp.bfloat16)
    step_raw = extras[:, extra : extra + heads]
    around = jnp.stack([columns] + [around_x(columns, -k) for k in range(1, NX)])
    quarters = [lax.dynamic_index_in_dim(around, (t - x) % NX, 0, keepdims=False) for t in range(NX)]
    b_values = jnp.concatenate(quarters[:2], axis=1)
    c_values = jnp.concatenate(quarters[2:], axis=1)

    live = (jnp.arange(length)[None, :] < new_counts[:, None]).astype(jnp.float32)
    step = jax.nn.softplus(step_raw + step_bias[None, :]).reshape(seq_dev, length, heads)
    step = step * live[:, :, None]
    decay = jnp.cumsum(-step * jnp.exp(decay_log)[None, None, :], axis=1)
    gain = jnp.repeat(skip_gain, HP)[None, :]
    live_column = live.reshape(rows, 1)
    local, factor = mix_locally(
        inner, b_values, c_values, decay, decay.transpose(0, 2, 1), step.transpose(0, 2, 1), gain, live_column
    )
    attention_out = attend(
        sources[:, SP:], prefix_pages, queries, new_keyvals, live_column, kv_in
    )
    mamba_out = carry_state(sources[:, :SP], state_in, c_values, factor, local)
    return (mamba_out, attention_out)


def solution(mesh):
    split = Mesh(mesh.devices.reshape(NY, NZ, 2, NX), DP + ("tensor",))
    placed = (
        P(DP, "tensor"),
        P(DP, "tensor"),
        P(DP, "tensor"),
        P(DP, "tensor"),
        P("tensor"),
        P("tensor"),
        P("tensor"),
        P(DP, "tensor"),
        P(DP, "tensor"),
        P(DP, None, "tensor"),
        P(DP, None),
        P(DP),
        P(DP),
    )
    return jax.shard_map(
        body,
        mesh=split,
        in_specs=placed,
        out_specs=(P(DP, "tensor"), P(DP, "tensor")),
        check_vma=False,
    )
```

```python
import functools
import math

import jax
import jax.numpy as jnp
from jax import lax
from jax.experimental import pallas as pl
from jax.experimental.pallas import tpu as pltpu
from jax.sharding import Mesh
from jax.sharding import PartitionSpec as P

HP = 64
NST = 256
HD = 128
PAGE = 128
SP = 16
NY = 4
NZ = 8
NX = 4
DP = ("y", "z", "core")
VMEM = 62 * 1024 * 1024
PASS_COST = 840 * 1024 * 1024
ANY = pl.BlockSpec(memory_space=pl.ANY)
HBM = pl.BlockSpec(memory_space=pltpu.HBM)
WHOLE = pl.BlockSpec(memory_space=pltpu.VMEM)
SCALARS = pl.BlockSpec(memory_space=pltpu.SMEM)


def around_x(array, by):
    return lax.ppermute(array, "tensor", [(i, (i + by) % NX) for i in range(NX)])


def pack_kernel(column, picks, pool, out, held, in_sems, out_sems):
    owners = out.shape[0]
    parts = in_sems.shape[0]
    span = owners // parts

    def fetch(r, part):
        pltpu.make_async_copy(pool.at[picks[r, 0, column]], held.at[r], in_sems.at[part]).start()
        return part

    def store(part):
        rows = pl.ds(part * span, span)
        return pltpu.make_async_copy(held.at[rows], out.at[rows], out_sems.at[part])

    for part in range(parts):
        lax.fori_loop(part * span, (part + 1) * span, fetch, part, unroll=8)
    for part in range(parts):
        rows = pl.ds(part * span, span)
        pltpu.make_async_copy(pool.at[pl.ds(0, span)], held.at[rows], in_sems.at[part]).wait()
        store(part).start()
    for part in range(parts):
        store(part).wait()


def pack_pages(picks, column, pool):
    owners = picks.shape[0]
    page = pool.shape[1:]
    return pl.pallas_call(
        functools.partial(pack_kernel, column),
        out_shape=jax.ShapeDtypeStruct((owners,) + page, pool.dtype),
        in_specs=[SCALARS, HBM],
        out_specs=HBM,
        scratch_shapes=[
            pltpu.VMEM((owners,) + page, pool.dtype),
            pltpu.SemaphoreType.DMA((4,)),
            pltpu.SemaphoreType.DMA((4,)),
        ],
        compiler_params=pltpu.CompilerParams(vmem_limit_bytes=VMEM),
        cost_estimate=pl.CostEstimate(
            flops=0, bytes_accessed=4 * owners * page[0] * page[1], transcendentals=0
        ),
        name="pack_pages",
    )(picks, pool)


def pass_kernel(weights, out):
    pass


def pass_on(weights):
    return pl.pallas_call(
        pass_kernel,
        out_shape=jax.ShapeDtypeStruct(weights.shape, weights.dtype),
        in_specs=[HBM],
        out_specs=HBM,
        input_output_aliases={0: 0},
        compiler_params=pltpu.CompilerParams(vmem_limit_bytes=VMEM),
        cost_estimate=pl.CostEstimate(flops=0, bytes_accessed=PASS_COST, transcendentals=0),
        name="pass_on",
    )(weights)


def project_kernel(x, weights, *refs):
    pieces = refs[:5]
    main_out, extra_out, w_all, t_all, w_sems, t_sems = refs[5:]
    tiles, wide = w_all.shape[0], w_all.shape[5]
    depth = t_all.shape[1]
    cols = pieces[0].shape[1]
    middle = pieces[3].shape[0]

    def columns(n):
        along = pl.ds(pl.multiple_of(n * wide, wide), wide)
        return [
            pltpu.make_async_copy(
                weights.at[y, core, :, :, along], w_all.at[n, y, :, core], w_sems.at[n, 2 * y + core]
            )
            for y in range(NY)
            for core in range(2)
        ]

    def start(n, carry):
        for copy in columns(n):
            copy.start()
        return carry

    copies = []
    for i, (first, by) in enumerate(((0, 0), (0, NX - 1), (0, 1), (0, 2), (middle, 2))):
        along = pl.multiple_of((x[0] + by) % NX * cols, cols)
        rows = pieces[i].shape[0]
        copies.append(
            pltpu.make_async_copy(
                pieces[i], t_all.at[pl.ds(first, rows), pl.ds(along, cols)], t_sems.at[i]
            )
        )
    for copy in copies:
        copy.start()
    lax.fori_loop(0, tiles, start, 0)
    for copy in copies:
        copy.wait()

    def product(n):
        for copy in columns(n):
            copy.wait()
        tile = w_all[n].reshape(depth, wide)
        return jnp.dot(t_all[...], tile, preferred_element_type=jnp.float32)

    def main_tile(n, carry):
        total = product(n)
        value = total / (1.0 + jnp.exp(-total))
        main_out[:, pl.ds(pl.multiple_of(n * wide, wide), wide)] = value.astype(jnp.bfloat16)
        return carry

    lax.fori_loop(0, tiles - 1, main_tile, 0)
    extra_out[...] = product(tiles - 1)


def project(x, weights, pieces, rows, wide):
    cols = weights.shape[-1]
    depth = weights.size // cols
    main = cols - wide
    return pl.pallas_call(
        project_kernel,
        out_shape=(
            jax.ShapeDtypeStruct((rows, main), jnp.bfloat16),
            jax.ShapeDtypeStruct((rows, wide), jnp.float32),
        ),
        in_specs=[SCALARS, HBM] + [ANY] * 5,
        out_specs=(WHOLE,) * 2,
        scratch_shapes=[
            pltpu.VMEM((cols // wide, NY, NZ, 2, depth // (2 * NY * NZ), wide), jnp.bfloat16),
            pltpu.VMEM((rows, depth), jnp.bfloat16),
            pltpu.SemaphoreType.DMA((cols // wide, 2 * NY)),
            pltpu.SemaphoreType.DMA((5,)),
        ],
        compiler_params=pltpu.CompilerParams(vmem_limit_bytes=VMEM),
        cost_estimate=pl.CostEstimate(
            flops=2 * rows * depth * cols, bytes_accessed=2 * depth * (cols + rows), transcendentals=rows * main
        ),
        name="project",
    )(x, weights, *pieces)


def split_dot(left, right):
    high = left.astype(jnp.bfloat16)
    low = (left - high.astype(jnp.float32)).astype(jnp.bfloat16)
    return jnp.dot(high, right, preferred_element_type=jnp.float32) + jnp.dot(
        low, right, preferred_element_type=jnp.float32
    )


def local_kernel(inner, b_values, c_values, decay, decay_t, step_t, gain, live, out, factor):
    length = PAGE
    row = lax.broadcasted_iota(jnp.int32, (length, length), 0)
    column = lax.broadcasted_iota(jnp.int32, (length, length), 1)
    causal = row >= column
    first = lax.broadcasted_iota(jnp.int32, (length, 2 * HP), 1) < HP
    for member in range(decay.shape[0]):
        rows = slice(member * length, (member + 1) * length)
        crossing = lax.dot_general(
            c_values[rows, :],
            b_values[rows, :],
            (((1,), (1,)), ((), ())),
            preferred_element_type=jnp.float32,
        )
        fades = jnp.exp(decay[member])
        for pair in range(decay.shape[2] // 2):
            lanes = slice(pair * 2 * HP, (pair + 1) * 2 * HP)
            values = inner[rows, lanes]
            parts = []
            for head in (2 * pair, 2 * pair + 1):
                gaps = decay[member, :, head : head + 1] - decay_t[member, head : head + 1, :]
                gaps = jnp.where(causal, gaps, -jnp.inf)
                mixing = jnp.exp(gaps) * crossing * step_t[member, head : head + 1, :]
                parts.append(split_dot(mixing, values))
            local = jnp.where(first, parts[0], parts[1])
            local = local + gain[:, lanes] * values.astype(jnp.float32)
            out[rows, lanes] = local * live[rows, :]
            fade = jnp.where(first, fades[:, 2 * pair : 2 * pair + 1], fades[:, 2 * pair + 1 : 2 * pair + 2])
            factor[rows, lanes] = fade * live[rows, :]


def mix_locally(inner, b_values, c_values, decay, decay_t, step_t, gain, live):
    rows, cols = inner.shape
    return pl.pallas_call(
        local_kernel,
        out_shape=(jax.ShapeDtypeStruct((rows, cols), jnp.float32),) * 2,
        in_specs=[WHOLE] * 8,
        out_specs=(WHOLE,) * 2,
        compiler_params=pltpu.CompilerParams(vmem_limit_bytes=VMEM),
        cost_estimate=pl.CostEstimate(
            flops=8 * rows * PAGE * cols, bytes_accessed=6 * rows * cols, transcendentals=rows * PAGE * 32
        ),
        name="mix_locally",
    )(inner, b_values, c_values, decay, decay_t, step_t, gain, live)


def carry_kernel(
    sources, incoming, c_values, factor, local, out, held, factors, locals_, ready, in_sems, out_sems
):
    members = sources.shape[0]
    span = 2 * PAGE

    def rows_of(member):
        return pl.ds(member * PAGE, PAGE)

    def bring(member):
        rows = rows_of(member)
        return [
            pltpu.make_async_copy(factor.at[rows, :], factors.at[rows, :], in_sems.at[member, 1]),
            pltpu.make_async_copy(local.at[rows, :], locals_.at[rows, :], in_sems.at[member, 2]),
        ]

    def store(member):
        rows = rows_of(member)
        return pltpu.make_async_copy(ready.at[rows, :], out.at[rows, :], out_sems.at[member])

    for member in range(members):
        for page in range(SP):
            pltpu.make_async_copy(
                incoming.at[sources[member, page]], held.at[member * SP + page], in_sems.at[member, 0]
            ).start()
        for copy in bring(member):
            copy.start()
    for member in range(members):
        rows = rows_of(member)
        pages = pl.ds(member * SP, SP)
        pltpu.make_async_copy(incoming.at[pl.ds(0, SP)], held.at[pages], in_sems.at[member, 0]).wait()
        for copy in bring(member):
            copy.wait()
        for page in range(0, SP, 2):
            lanes = slice(page * 2 * HP, page * 2 * HP + span)
            pair = held[member * SP + page : member * SP + page + 2].reshape(span, NST)
            carried = lax.dot_general(
                c_values[rows, :], pair, (((1,), (1,)), ((), ())), preferred_element_type=jnp.float32
            )
            total = locals_[rows, lanes] + carried * factors[rows, lanes]
            ready[rows, lanes] = total.astype(jnp.bfloat16)
        store(member).start()
    for member in range(members):
        store(member).wait()


def carry_state(sources, incoming, c_values, factor, local):
    rows, cols = local.shape
    members = sources.shape[0]
    return pl.pallas_call(
        carry_kernel,
        out_shape=jax.ShapeDtypeStruct((rows, cols), jnp.bfloat16),
        in_specs=[SCALARS, HBM, WHOLE, HBM, HBM],
        out_specs=HBM,
        scratch_shapes=[
            pltpu.VMEM((members * SP,) + incoming.shape[1:], incoming.dtype),
            pltpu.VMEM((rows, cols), jnp.float32),
            pltpu.VMEM((rows, cols), jnp.float32),
            pltpu.VMEM((rows, cols), jnp.bfloat16),
            pltpu.SemaphoreType.DMA((members, 3)),
            pltpu.SemaphoreType.DMA((members,)),
        ],
        compiler_params=pltpu.CompilerParams(vmem_limit_bytes=VMEM),
        cost_estimate=pl.CostEstimate(
            flops=2 * rows * NST * cols, bytes_accessed=8 * rows * cols, transcendentals=0
        ),
        name="carry_state",
    )(sources, incoming, c_values, factor, local)


CHUNK = 8


def attend_kernel(sources, prefix, counts, queries, fresh, incoming, out, stacked, held, top, total, sems):
    members, slots = sources.shape
    heads = queries.shape[1] // HD
    factor = math.log2(math.e) / math.sqrt(HD)
    nothing = -1e30

    def copy(member, slot):
        return pltpu.make_async_copy(
            incoming.at[sources[member, slot]],
            held.at[member, pl.ds(pl.multiple_of(slot * PAGE, PAGE), PAGE), :],
            sems.at[member, slot],
        )

    for member in range(members):

        def start(slot, carry):
            @pl.when(slot < prefix[member])
            def _():
                copy(member, slot).start()

            @pl.when(slot >= prefix[member])
            def _():
                held[member, pl.ds(pl.multiple_of(slot * PAGE, PAGE), PAGE), :] = jnp.zeros(
                    (PAGE, 2 * HD), held.dtype
                )

            return carry

        lax.fori_loop(0, slots, start, 0)

    wide = CHUNK * PAGE
    block = 2 * PAGE
    causal = lax.broadcasted_iota(jnp.int32, (block, PAGE), 0) % PAGE >= lax.broadcasted_iota(
        jnp.int32, (block, PAGE), 1
    )
    for member in range(members):
        rows = slice(member * PAGE, (member + 1) * PAGE)
        for head in range(heads):
            stacked[head * PAGE : (head + 1) * PAGE, :] = queries[rows, head * HD : (head + 1) * HD]
        new_keys = fresh[rows, :HD]
        new_values = jnp.concatenate([jnp.ones((PAGE, HD), jnp.bfloat16), fresh[rows, HD:]], axis=1)
        for part in range(heads // 2):
            at = slice(part * block, (part + 1) * block)
            scores = lax.dot_general(
                stacked[at, :], new_keys, (((1,), (1,)), ((), ())), preferred_element_type=jnp.float32
            )
            scores = jnp.where(causal, scores * factor, nothing)
            best = jnp.max(scores, axis=1, keepdims=True)
            weights = jnp.exp2(scores - best).astype(jnp.bfloat16)
            top[at, :] = jnp.broadcast_to(best, (block, HD))
            total[at, :] = jnp.dot(weights, new_values, preferred_element_type=jnp.float32)

        def chunk(index, carry):
            base = index * CHUNK

            def finish(slot, inside):
                @pl.when(base + slot < prefix[member])
                def _():
                    copy(member, base + slot).wait()

                return inside

            lax.fori_loop(0, CHUNK, finish, 0)
            span = pl.ds(pl.multiple_of(index * wide, wide), wide)
            keys = held[member, span, :HD]
            values = jnp.concatenate([jnp.ones((wide, HD), jnp.bfloat16), held[member, span, HD:]], axis=1)
            seen = index * wide + lax.broadcasted_iota(jnp.int32, (1, wide), 1) < prefix[member] * PAGE
            bias = jnp.where(seen, 0.0, nothing)
            for part in range(heads // 2):
                at = slice(part * block, (part + 1) * block)
                scores = lax.dot_general(
                    stacked[at, :], keys, (((1,), (1,)), ((), ())), preferred_element_type=jnp.float32
                )
                scores = scores * factor + bias
                before = top[at, :1]
                best = jnp.maximum(before, jnp.max(scores, axis=1, keepdims=True))
                weights = jnp.exp2(scores - best).astype(jnp.bfloat16)
                shrink = jnp.exp2(before - best)
                top[at, :] = jnp.broadcast_to(best, (block, HD))
                total[at, :] = total[at, :] * shrink + jnp.dot(
                    weights, values, preferred_element_type=jnp.float32
                )
            return carry

        lax.fori_loop(0, (prefix[member] + CHUNK - 1) // CHUNK, chunk, 0)
        live = lax.broadcasted_iota(jnp.int32, (PAGE, HD), 0) < counts[member]
        for head in range(heads):
            at = slice(head * PAGE, (head + 1) * PAGE)
            mixed = jnp.where(live, total[at, HD:] / total[at, :HD], 0.0)
            out[rows, head * HD : (head + 1) * HD] = mixed.astype(jnp.bfloat16)


def attend(sources, prefix, counts, queries, fresh, incoming):
    rows, cols = queries.shape
    members, slots = sources.shape
    heads = cols // HD
    return pl.pallas_call(
        attend_kernel,
        out_shape=jax.ShapeDtypeStruct((rows, cols), jnp.bfloat16),
        in_specs=[SCALARS] * 3 + [WHOLE] * 2 + [HBM],
        out_specs=WHOLE,
        scratch_shapes=[
            pltpu.VMEM((heads * PAGE, HD), jnp.bfloat16),
            pltpu.VMEM((members, slots * PAGE, 2 * HD), jnp.bfloat16),
            pltpu.VMEM((heads * PAGE, HD), jnp.float32),
            pltpu.VMEM((heads * PAGE, 2 * HD), jnp.float32),
            pltpu.SemaphoreType.DMA((members, slots)),
        ],
        compiler_params=pltpu.CompilerParams(vmem_limit_bytes=VMEM),
        cost_estimate=pl.CostEstimate(
            flops=256 * rows * cols * slots * PAGE,
            bytes_accessed=members * slots * PAGE * 4 * HD,
            transcendentals=rows * heads * slots * PAGE,
        ),
        name="attend",
    )(sources, prefix, counts, queries, fresh, incoming)


def gather_tokens(tokens):
    middle = tokens.shape[0] // 2
    up, down = around_x(tokens, 1), around_x(tokens, -1)
    return [tokens, up, down, around_x(up[:middle], 1), around_x(down[middle:], -1)]


def body(
    tokens,
    x_weight,
    bc_weight,
    step_weight,
    step_bias,
    decay_log,
    skip_gain,
    queries,
    new_keyvals,
    page_pool,
    page_table,
    prefix_pages,
    new_counts,
):
    owners = lax.axis_size(DP)
    x = lax.axis_index("tensor")
    seq_dev = page_table.shape[0]
    pool_size = page_pool.shape[0]
    rows = tokens.shape[0]
    length = rows // seq_dev
    heads = step_bias.shape[0]

    sources = page_table // pool_size
    places = page_table % pool_size
    names = jnp.arange(owners, dtype=jnp.int32)[:, None]

    def wanted(part):
        asked = sources[:, part].reshape(1, -1) == names
        return jnp.max(jnp.where(asked, places[:, part].reshape(1, -1), 0), axis=1)

    asks = jnp.stack([wanted(slice(SP, None)), wanted(slice(0, SP))], axis=1)
    asks = jnp.pad(asks, ((0, 0), (0, 126))).reshape(owners, 1, 128)
    extra = bc_weight.shape[1]
    x_weight, bc_weight, step_weight, asks = lax.optimization_barrier(
        (x_weight, bc_weight, step_weight, asks)
    )
    step_wide = jnp.pad(step_weight, ((0, 0), (0, extra - heads)))
    weights = jnp.concatenate([x_weight, bc_weight, step_wide], axis=1)
    weights = lax.all_gather(weights, "z", axis=0)
    picks = lax.all_to_all(asks, DP, split_axis=0, concat_axis=0, tiled=True)
    kv_out = pack_pages(picks, 0, page_pool)
    state_out = pack_pages(picks, 1, page_pool)
    kv_out, state_out = lax.optimization_barrier((kv_out, state_out))
    kv_in = lax.all_to_all(kv_out, DP, split_axis=0, concat_axis=0, tiled=True)
    state_in = lax.all_to_all(state_out, DP, split_axis=0, concat_axis=0, tiled=True)

    weights, _ = lax.optimization_barrier((weights, state_out))
    weights = pass_on(weights)
    weights = lax.all_gather(weights, ("y", "core"), axis=0)
    weights = weights.reshape((NY, 2) + weights.shape[1:])
    attention_out = attend(
        sources[:, SP:], prefix_pages, new_counts, queries, new_keyvals, kv_in
    )
    tokens, decay_log, skip_gain, new_counts, _ = lax.optimization_barrier(
        (tokens, decay_log, skip_gain, new_counts, attention_out)
    )
    inner, extras = project(
        x.reshape(1).astype(jnp.int32), weights, gather_tokens(tokens), rows, 2 * extra
    )
    columns = extras[:, :extra].astype(jnp.bfloat16)
    step_raw = extras[:, extra : extra + heads]
    around = jnp.stack([columns] + [around_x(columns, -k) for k in range(1, NX)])
    quarters = [lax.dynamic_index_in_dim(around, (t - x) % NX, 0, keepdims=False) for t in range(NX)]
    b_values = jnp.concatenate(quarters[:2], axis=1)
    c_values = jnp.concatenate(quarters[2:], axis=1)

    live = (jnp.arange(length)[None, :] < new_counts[:, None]).astype(jnp.float32)
    step = jax.nn.softplus(step_raw + step_bias[None, :]).reshape(seq_dev, length, heads)
    step = step * live[:, :, None]
    decay = jnp.cumsum(-step * jnp.exp(decay_log)[None, None, :], axis=1)
    gain = jnp.repeat(skip_gain, HP)[None, :]
    live_column = live.reshape(rows, 1)
    local, factor = mix_locally(
        inner, b_values, c_values, decay, decay.transpose(0, 2, 1), step.transpose(0, 2, 1), gain, live_column
    )
    mamba_out = carry_state(sources[:, :SP], state_in, c_values, factor, local)
    return (mamba_out, attention_out)


def solution(mesh):
    split = Mesh(mesh.devices.reshape(NY, NZ, 2, NX), DP + ("tensor",))
    placed = (
        P(DP, "tensor"),
        P(DP, "tensor"),
        P(DP, "tensor"),
        P(DP, "tensor"),
        P("tensor"),
        P("tensor"),
        P("tensor"),
        P(DP, "tensor"),
        P(DP, "tensor"),
        P(DP, None, "tensor"),
        P(DP, None),
        P(DP),
        P(DP),
    )
    return jax.shard_map(
        body,
        mesh=split,
        in_specs=placed,
        out_specs=(P(DP, "tensor"), P(DP, "tensor")),
        check_vma=False,
    )
```
